32 devices in a mesh: dp: 8 (over z, y), tensor: 4 (over x, core).
Axes of the slice: x: 2, y: 2, z: 4, core: 2. Of those that a mesh axis runs over, the one named last changes fastest.
Arguments:
- tokens: bfloat16 [584, 16, 1024], P('tensor', 'dp'), may hold values from -6 to 6
- valid_mask: int32 [584, 16], P(None, 'dp'), may hold values from 0 to 1, as said below
- teacher: bfloat16 [584, 16, 1024], P('tensor', 'dp'), may hold values from -6 to 6
- loss_scale: float32 [], replicated, may hold values from 2363392 to 4726784
- ln1_gain: float32 [1024], replicated, may hold values from 0.5 to 1.5
- ln1_shift: float32 [1024], replicated, may hold values from -0.3 to 0.3
- w_qkv: bfloat16 [1024, 3, 1024], P('dp', None, 'tensor'), may hold values from -0.1875 to 0.1875
- b_qv: float32 [2, 1024], replicated, may hold values from -0.3 to 0.3
- w_out: bfloat16 [1024, 1024], P('tensor', 'dp'), may hold values from -1 to 1
- b_out: float32 [1024], replicated, may hold values from -0.3 to 0.3
- ln2_gain: float32 [1024], replicated, may hold values from 0.5 to 1.5
- ln2_shift: float32 [1024], replicated, may hold values from -0.3 to 0.3
- w_fc1: bfloat16 [1024, 4096], P('dp', 'tensor'), may hold values from -0.1875 to 0.1875
- b_fc1: float32 [4096], replicated, may hold values from -0.3 to 0.3
- w_fc2: bfloat16 [4096, 1024], P('tensor', 'dp'), may hold values from -0.09375 to 0.09375
- b_fc2: float32 [1024], replicated, may hold values from -0.3 to 0.3
Outputs:
- out: bfloat16 [584, 16, 1024], P('tensor', 'dp')
- loss: float32 [], replicated
- grad_tokens: float32 [584, 16, 1024], P('tensor', 'dp')
- grad_ln1_gain: float32 [1024], P(('dp', 'tensor'))
- grad_ln1_shift: float32 [1024], P(('dp', 'tensor'))
- grad_w_qkv: float32 [1024, 3, 1024], P('dp', None, 'tensor')
- grad_b_qv: float32 [2, 1024], P(None, ('dp', 'tensor'))
- grad_w_out: float32 [1024, 1024], P('tensor', 'dp')
- grad_b_out: float32 [1024], P(('dp', 'tensor'))
- grad_ln2_gain: float32 [1024], P(('dp', 'tensor'))
- grad_ln2_shift: float32 [1024], P(('dp', 'tensor'))
- grad_w_fc1: float32 [1024, 4096], P('dp', 'tensor')
- grad_b_fc1: float32 [4096], P(('dp', 'tensor'))
- grad_w_fc2: float32 [4096, 1024], P('tensor', 'dp')
- grad_b_fc2: float32 [1024], P(('dp', 'tensor'))
The draws below stay inside these ranges and needn't reach their ends.
Inputs may be any that keep to these rules, and one draw needn't show every extreme that they name: `valid_mask`: one image in eight, chosen at random, is padding and has no valid row; every other image is valid exactly at its first 577 rows.
All inputs are finite; a program needn't handle non-finite values.
Results may differ from the reference program's by a relative error of at most 0.013.
Values may be sent and summed in bfloat16 or wider, within the bound.
A program may use at most 128 MiB of HBM per device.

```python
import math
import jax
import jax.numpy as jnp
from jax import lax

D = 1024
H = 16
HD = 64
FF = 4096
TOK = 577
SEQ = 584
IMG_DEV = 2
IMAGES = 16


def draw_valid_mask(key, part):
    order = jax.random.permutation(jax.random.fold_in(key, 7), IMAGES)
    real_image = order >= IMAGES // 8
    real_row = jnp.arange(SEQ) < TOK
    return (real_row[:, None] & real_image[None, :]).astype(jnp.int32)


def block_levels(own_key, extent, shards, least, largest):
    loudness = 1.0
    for position, parts in shards:
        heights = jax.random.uniform(jax.random.fold_in(jax.random.fold_in(own_key, 6), position), (parts,), jnp.float32, least / len(shards), largest / len(shards))
        loudness = loudness * jnp.repeat(jnp.exp(heights), extent[position] // parts).reshape((-1,) + (1,) * (len(extent) - 1 - position))
    return loudness


def gaussian(key, dims, scale, bound, cuts=(), dtype=jnp.bfloat16):
    level = block_levels(key, dims, cuts, -0.22, 0.18) if cuts else 1.0
    entries = jax.random.normal(key, dims, jnp.float32) * scale * level
    return jnp.minimum(jnp.maximum(entries, -bound), bound).astype(dtype)


def setup_inputs(seed: int = 0) -> dict:
    splits = jax.random.split(jax.random.key(seed), 17)
    tokens = gaussian(splits[0], (SEQ, IMAGES, D), 1.0, 6.0, ((0, 4), (1, 8)))
    valid_mask = draw_valid_mask(jax.random.fold_in(splits[16], 71), 0)
    teacher = gaussian(splits[2], (SEQ, IMAGES, D), 1.0, 6.0, ((0, 4), (1, 8)))
    loss_scale = jnp.clip(jnp.exp(jax.random.uniform(splits[3], (), jnp.float32, math.log(2363392), math.log(4726784))), 2363392, 4726784)
    ln1_gain = jnp.clip(1.0 + 0.1 * jax.random.normal(splits[4], (D,), jnp.float32), 0.5, 1.5)
    ln1_shift = gaussian(splits[5], (D,), 0.05, 0.3, (), jnp.float32)
    w_qkv = gaussian(splits[6], (D, 3, D), D ** -0.5, 0.1875, ((0, 8), (2, 4)))
    b_qv = gaussian(splits[7], (2, D), 0.05, 0.3, (), jnp.float32)
    w_out = gaussian(splits[8], (D, D), (D // 24) ** -0.5, 1.0, ((0, 4), (1, 8)))
    b_out = gaussian(splits[9], (D,), 0.05, 0.3, (), jnp.float32)
    ln2_gain = jnp.clip(1.0 + 0.1 * jax.random.normal(splits[10], (D,), jnp.float32), 0.5, 1.5)
    ln2_shift = gaussian(splits[11], (D,), 0.05, 0.3, (), jnp.float32)
    w_fc1 = gaussian(splits[12], (D, FF), D ** -0.5, 0.1875, ((0, 8), (1, 4)))
    b_fc1 = gaussian(splits[13], (FF,), 0.05, 0.3, (), jnp.float32)
    w_fc2 = gaussian(splits[14], (FF, D), FF ** -0.5, 0.09375, ((0, 4), (1, 8)))
    b_fc2 = gaussian(splits[15], (D,), 0.05, 0.3, (), jnp.float32)
    return dict(tokens=tokens, valid_mask=valid_mask, teacher=teacher, loss_scale=loss_scale, ln1_gain=ln1_gain, ln1_shift=ln1_shift, w_qkv=w_qkv, b_qv=b_qv, w_out=w_out, b_out=b_out, ln2_gain=ln2_gain, ln2_shift=ln2_shift, w_fc1=w_fc1, b_fc1=b_fc1, w_fc2=w_fc2, b_fc2=b_fc2)


@jax.custom_vjp
def low(v):
    return lax.optimization_barrier(v.astype(jnp.bfloat16)).astype(jnp.float32)

@jax.custom_vjp
def low_back(v):
    return v

def low_keep(v):
    return (low(v), None)

def low_pass(kept, grad):
    return (grad,)

def back_keep(v):
    return (v, None)

def back_low(kept, grad):
    return (low(grad),)
low.defvjp(low_keep, low_pass)
low_back.defvjp(back_keep, back_low)
epsilon = 1e-05
masked_score = -1000000000.0
gelu_factor = 1.702
highest = lax.Precision.HIGHEST

def layer_norm(values, gain, shift):
    center = values - lax.optimization_barrier(jnp.mean(values, axis=-1, keepdims=True))
    inverse = lax.rsqrt(lax.optimization_barrier(jnp.mean(center * center, axis=-1, keepdims=True)) + epsilon)
    return center * inverse * gain + shift

def attend(pieces):
    query, key, value, keep = pieces
    scores = jnp.einsum('qhe,khe->hqk', query, key, precision=highest) * HD ** (-0.5)
    scores = jnp.where(keep[None, None, :] > 0, low_back(scores), masked_score)
    probs = jax.nn.softmax(scores, axis=-1)
    return jnp.einsum('hqk,khe->qhe', low(probs), value, precision=highest)

def block(inputs, valid, teacher, count, ln1_gain, ln1_shift, w_qkv, b_qv, w_out, b_out, ln2_gain, ln2_shift, w_fc1, b_fc1, w_fc2, b_fc2):
    full_rows = inputs.shape[0]
    images = inputs.shape[1]
    normed1 = low(layer_norm(inputs, ln1_gain, ln1_shift))
    proj = jnp.einsum('sid,dce->sice', normed1, w_qkv, precision=highest)
    query = low(low_back(proj[:, :, 0] + b_qv[0]))
    key = low(low_back(proj[:, :, 1]))
    value = low(low_back(proj[:, :, 2] + b_qv[1]))

    def heads_first(values):
        return jnp.moveaxis(values.reshape(full_rows, images, H, HD), 1, 0)
    mixed = lax.map(jax.checkpoint(attend), (heads_first(query), heads_first(key), heads_first(value), jnp.transpose(valid)))
    attended = low(low_back(jnp.moveaxis(mixed, 0, 1).reshape(full_rows, images, D)))
    attn_sum = low_back(jnp.einsum('sie,ed->sid', attended, w_out, precision=highest))
    middle = inputs + attn_sum + b_out
    normed2 = low(layer_norm(middle, ln2_gain, ln2_shift))
    pre = low_back(jnp.einsum('sid,df->sif', normed2, w_fc1, precision=highest) + b_fc1)
    act = low(pre * jax.nn.sigmoid(gelu_factor * pre))
    mlp_sum = low_back(jnp.einsum('sif,fd->sid', act, w_fc2, precision=highest))
    final = middle + mlp_sum + b_fc2
    difference = final - teacher
    loss_part = jnp.sum(valid[:, :, None] * difference * difference) / (count * D)
    return (loss_part, final)

def reference(tokens, valid_mask, teacher, loss_scale, ln1_gain, ln1_shift, w_qkv, b_qv, w_out, b_out, ln2_gain, ln2_shift, w_fc1, b_fc1, w_fc2, b_fc2):
    valid = valid_mask.astype(jnp.float32)
    count = jnp.sum(valid)
    params = (ln1_gain, ln1_shift, w_qkv.astype(jnp.float32), b_qv, w_out.astype(jnp.float32), b_out, ln2_gain, ln2_shift, w_fc1.astype(jnp.float32), b_fc1, w_fc2.astype(jnp.float32), b_fc2)
    groups = IMAGES // IMG_DEV
    token_groups = jnp.moveaxis(tokens.astype(jnp.float32).reshape(SEQ, groups, IMG_DEV, D), 1, 0)
    teacher_groups = jnp.moveaxis(teacher.astype(jnp.float32).reshape(SEQ, groups, IMG_DEV, D), 1, 0)
    valid_groups = jnp.moveaxis(valid.reshape(SEQ, groups, IMG_DEV), 1, 0)

    def step(carry, pieces):
        inputs, valid_part, teacher_part = pieces

        def loss_of(inputs_in, *weights):
            return block(inputs_in, valid_part, teacher_part, count, *weights)
        loss_part, pullback, final = jax.vjp(loss_of, inputs, *params, has_aux=True)
        grads = pullback(loss_scale)
        sums = tuple((earlier + later for earlier, later in zip(carry[1], grads[1:])))
        return ((carry[0] + loss_part, sums), (final.astype(jnp.bfloat16), grads[0]))
    start = (jnp.zeros((), jnp.float32), tuple((jnp.zeros_like(param) for param in params)))
    (loss, sums), (finals, grad_groups) = lax.scan(step, start, (token_groups, valid_groups, teacher_groups))
    out = jnp.moveaxis(finals, 0, 1).reshape(SEQ, IMAGES, D)
    grad_tokens = jnp.moveaxis(grad_groups, 0, 1).reshape(SEQ, IMAGES, D)
    return (out, loss, grad_tokens, sums[0], sums[1], sums[2], sums[3], sums[4], sums[5], sums[6], sums[7], sums[8], sums[9], sums[10], sums[11])
```

```python
import functools

import jax
import jax.numpy as jnp
from jax import lax
from jax.experimental import pallas as pl
from jax.experimental.pallas import tpu as pltpu
from jax.sharding import PartitionSpec as P

HD = 64
EPS = 1e-05
MASKED = -1000000000.0
PADDED = -3000000000.0
GELU = 1.702
MESH = pl.DeviceIdType.MESH
f32 = jnp.float32
bf16 = jnp.bfloat16
NN = (((1,), (0,)), ((), ()))
NT = (((1,), (1,)), ((), ()))
TN = (((0,), (0,)), ((), ()))

LN1G, LN1S, LN2G, LN2S, BOUT, BFC2, BFC1, BQKV, LSC, CNT = range(10)


def dot(a, b, dims):
    return lax.dot_general(a, b, dims, preferred_element_type=f32)


def layer_norm(values, gain, shift):
    center = values - jnp.mean(values, axis=-1, keepdims=True)
    inverse = lax.rsqrt(jnp.mean(center * center, axis=-1, keepdims=True) + EPS)
    scaled = center * inverse
    return scaled * gain + shift, scaled, inverse


def norm_backward(upstream, scaled, inverse, gain):
    weighted = upstream * gain
    inner = weighted - jnp.mean(weighted, axis=-1, keepdims=True)
    inner = inner - scaled * jnp.mean(weighted * scaled, axis=-1, keepdims=True)
    return inverse * inner


def rowsum(values):
    return jnp.sum(values, axis=0, keepdims=True)


def aligned(start, size):
    return pl.ds(pl.multiple_of(start, size), size)


class Copies:
    def __init__(self, send, recv):
        self.send, self.recv, self.count = send, recv, 0
        self.all = []

    def make(self, src, dst, device):
        copy = pltpu.make_async_remote_copy(
            src_ref=src,
            dst_ref=dst,
            send_sem=self.send.at[self.count],
            recv_sem=self.recv.at[self.count],
            device_id=device,
            device_id_type=MESH,
        )
        self.count += 1
        return copy

    def start(self, src, dst, device):
        copy = self.make(src, dst, device)
        copy.start()
        self.all.append(copy)
        return copy

    def wait_send(self, copy):
        copy.wait_send()
        self.all = [other for other in self.all if other is not copy]

    def finish(self):
        for copy in self.all:
            copy.wait_send()
        self.all = []


def kernel(
    size,
    tok, tea, rmask, keep, vec, wq, wo, w1, w2,
    out, gtok, gq, go, g1, g2, vecE, vecL,
    Wq, Wo, W1, W2, N1, N2, N3, N4, QKV, PR, ATT, ACT, DAC, GA, GP, PART, RA, RX, XS, MID, DIF,
    GWq, GWo, GW1, GW2, YRq, YRo, YR1, YR2, ZRq, ZRo, ZR1, ZR2,
    USUM, VE, VL, CN, local_sem, send_sem, recv_sem,
):
    I, LR, IR, D, HC, UC = size["I"], size["LR"], size["IR"], size["D"], size["HC"], size["UC"]
    inside = size["inside"]
    KS = size["KS"]
    dp, tensor = lax.axis_index("dp"), lax.axis_index("tensor")
    z, y, x, c = dp // 2, dp % 2, tensor // 2, tensor % 2
    mate = (dp, x * 2 + 1 - c)
    xnei = (dp, (1 - x) * 2 + c)
    ynei = (z * 2 + 1 - y, tensor)

    def zdev(k):
        return (lax.rem(z + k, 4) * 2 + y, tensor)

    net = Copies(send_sem, recv_sem)

    barrier = pltpu.get_barrier_semaphore()
    peers = [mate, xnei] + ([ynei] + [zdev(k) for k in (1, 2, 3)] if inside else [])
    for peer in peers:
        pl.semaphore_signal(barrier, inc=1, device_id=peer, device_id_type=MESH)
    pl.semaphore_wait(barrier, len(peers))

    weights = [(wq, Wq, 0, YRq, ZRq, GWq, gq), (wo, Wo, 1, YRo, ZRo, GWo, go),
               (w1, W1, 0, YR1, ZR1, GW1, g1), (w2, W2, 1, YR2, ZR2, GW2, g2)]

    def shard(ref, axis, index):
        place = pl.ds(pl.multiple_of(index * KS, KS), KS)
        return ref.at[place, :] if axis == 0 else ref.at[:, place]

    gathers = {}
    locals_ = []

    def weight_send(w):
        arg, full, axis = weights[w][:3]
        if not inside:
            copy = pltpu.make_async_copy(arg, full, local_sem.at[w])
            copy.start()
            locals_.append(copy)
            return
        mine = shard(full, axis, dp)
        copy = pltpu.make_async_copy(arg, mine, local_sem.at[w])
        copy.start()
        locals_.append(copy)
        zs = [net.start(arg, mine, zdev(k)) for k in (1, 2, 3)]
        ys = [net.start(arg, mine, ynei)]
        gathers[w] = (zs, ys)

    def weight_forward(w):
        if not inside:
            return
        arg, full, axis = weights[w][:3]
        zs, ys = gathers[w]
        for k in (1, 2, 3):
            zs[k - 1].wait_recv()
            got = shard(full, axis, lax.rem(z + 4 - k, 4) * 2 + y)
            ys.append(net.start(got, got, ynei))

    def weight_wait(w):
        locals_[w].wait()
        if inside:
            for copy in gathers[w][1]:
                copy.wait_recv()

    scatters = {}

    def grad_y(w):
        if not inside:
            return
        axis, YR, GW = weights[w][2], weights[w][3], weights[w][5]
        ys = []
        for k in (1, 2, 3, 0):
            ys.append(net.start(shard(GW, axis, lax.rem(z + k, 4) * 2 + 1 - y), YR.at[k], ynei))
        scatters[w] = ys

    def grad_z(w):
        if not inside:
            return
        axis, YR, ZR, GW = weights[w][2:6]
        zs = []
        for n, k in enumerate((1, 2, 3)):
            scatters[w][n].wait_recv()
            place = shard(GW, axis, lax.rem(z + k, 4) * 2 + y)
            place[...] = (place[...].astype(f32) + YR[k].astype(f32)).astype(bf16)
            zs.append(net.start(place, ZR.at[k - 1], zdev(k)))
        scatters[w].append(zs)

    def grad_end(w):
        axis, YR, ZR, GW, result = weights[w][2:7]
        if not inside:
            result[...] = GW[...]
            return
        scatters[w][3].wait_recv()
        total = shard(GW, axis, dp)[...].astype(f32) + YR[0].astype(f32)
        for k in (1, 2, 3):
            scatters[w][4][k - 1].wait_recv()
            total = total + ZR[k - 1].astype(f32)
        result[...] = total

    def vector_sum(V, rows):
        own, got = 0, 1
        copy = net.start(V.at[0], V.at[1], mate)
        copy.wait_recv()
        V[2] = V[0] + V[1]
        copy = net.start(V.at[2], V.at[3], xnei)
        copy.wait_recv()
        if not inside:
            V[4] = V[2] + V[3]
            return V[4]
        V[4 + z] = V[2] + V[3]
        copies = [net.start(V.at[4 + z], V.at[4 + z], zdev(k)) for k in (1, 2, 3)]
        for copy in copies:
            copy.wait_recv()
        V[8] = (V[4] + V[5]) + (V[6] + V[7])
        copy = net.start(V.at[8], V.at[9], ynei)
        copy.wait_recv()
        return V[8] + V[9]

    def count_start():
        if not inside:
            return None
        CN[z] = jnp.broadcast_to(jnp.sum(keep[0:I, :], keepdims=True), (8, 128))
        return [net.start(CN.at[z], CN.at[z], zdev(k)) for k in (1, 2, 3)]

    def count_next(copies):
        if not inside:
            return None
        for copy in copies:
            copy.wait_recv()
        CN[4] = (CN[0] + CN[1]) + (CN[2] + CN[3])
        return net.start(CN.at[4], CN.at[5], ynei)

    def count_end(copy):
        if not inside:
            return vec[CNT:CNT + 1, 0:1]
        copy.wait_recv()
        return CN[4, 0:1, 0:1] + CN[5, 0:1, 0:1]

    def block(i, t):
        return aligned((i * 4 + t) * LR, LR)

    def local(i):
        return pl.ds(i * LR, LR)

    def pair(i, xx):
        return aligned(i * IR + xx * 2 * LR, 2 * LR)

    own_t, other_t = tensor, (1 - x) * 2 + c
    ag, rs = {}, {}

    def ag_start(s, N, i):
        mine = N.at[block(i, own_t), :]
        ag[s, i] = [net.start(mine, mine, xnei), net.start(mine, mine, mate)]

    def ag_forward(s, N, i):
        ag[s, i][0].wait_recv()
        got = N.at[block(i, other_t), :]
        ag[s, i].append(net.start(got, got, mate))

    def ag_wait(s, i):
        ag[s, i][1].wait_recv()
        ag[s, i][2].wait_recv()

    def landing(ref, n):
        return ref.at[pl.ds(n * LR, LR), :]

    def rs_ready(s, i):
        if s:
            for copy in rs[s - 1, i][:2]:
                net.wait_send(copy)

    def rs_send(s, i, far):
        base = i * IR + ((1 - x) if far else x) * 2 * LR
        src = PART.at[aligned(base + (1 - c) * LR, LR), :]
        rs.setdefault((s, i), []).append(net.start(src, landing(RA, i * 2 + (0 if far else 1)), mate))

    def rs_mid(s, i):
        rs[s, i][0].wait_recv()
        if s:
            net.wait_send(rs[s - 1, i][2])
        kept = PART[aligned(i * IR + (1 - x) * 2 * LR + c * LR, LR), :]
        XS[local(i), :] = (kept.astype(f32) + landing(RA, i * 2)[...].astype(f32)).astype(bf16)
        rs[s, i].append(net.start(XS.at[local(i), :], landing(RX, i), xnei))

    def rs_finish(s, i):
        rs[s, i][1].wait_recv()
        rs[s, i][2].wait_recv()
        kept = PART[aligned(i * IR + x * 2 * LR + c * LR, LR), :].astype(f32)
        return kept + landing(RA, i * 2 + 1)[...].astype(f32) + landing(RX, i)[...].astype(f32)

    def vrow(n, lo=0, hi=None):
        return vec[n:n + 1, lo:(D if hi is None else hi)]

    TC = 512 if D % 512 == 0 and UC % 512 == 0 else 256

    def over_columns(n, step, body):
        for j in range(n // step):
            body(pl.ds(j * step, step))

    def f_norm1(i):
        normed = layer_norm(tok[local(i), :].astype(f32), vrow(LN1G), vrow(LN1S))[0]
        N1[block(i, own_t), :] = normed.astype(bf16)
        ag_start(0, N1, i)

    lane_head = lax.broadcasted_iota(jnp.int32, (1, HC), 1) // HD
    zero = jnp.zeros((), bf16)

    def f_attention(i):
        rows = pl.ds(i * IR, IR)
        for n in range(3):
            def body(cols):
                proj = dot(N1[rows, :], Wq[:, cols], NN) + vec[BQKV:BQKV + 1, cols]
                if n == 0:
                    proj = proj.astype(bf16).astype(f32) * (HD ** -0.5)
                QKV[rows, cols] = proj.astype(bf16)
            body(pl.ds(n * HC, HC))
        acc = None
        for h in range(HC // HD):
            pick = lane_head == h
            keys = jnp.where(pick, QKV[rows, HC:2 * HC], zero)
            scores = dot(QKV[rows, 0:HC], keys, NT)
            scores = scores * keep[i:i + 1, :] + keep[I + i:I + i + 1, :]
            expo = jnp.exp(scores - jnp.max(scores, axis=-1, keepdims=True))
            probs = (expo * (1.0 / jnp.sum(expo, axis=-1, keepdims=True))).astype(bf16)
            PR[i * (HC // HD) + h] = probs
            values = jnp.where(pick, QKV[rows, 2 * HC:3 * HC], zero)
            part = dot(probs, values, NN)
            acc = part if acc is None else acc + part
        ATT[rows, :] = acc.astype(bf16)
        rs_ready(0, i)
        for far in (True, False):
            prow = pair(i, (1 - x) if far else x)
            def body(cols):
                PART[prow, cols] = dot(ATT[prow, :], Wo[:, cols], NN).astype(bf16)
            over_columns(D, TC, body)
            rs_send(0, i, far)

    def f_norm2(i):
        middle = tok[local(i), :].astype(f32) + rs_finish(0, i) + vrow(BOUT)
        MID[local(i), :] = middle
        N2[block(i, own_t), :] = layer_norm(middle, vrow(LN2G), vrow(LN2S))[0].astype(bf16)
        ag_start(1, N2, i)

    def f_feed(i):
        rows = pl.ds(i * IR, IR)
        ag_wait(1, i)
        def body(cols):
            pre = dot(N2[rows, :], W1[:, cols], NN) + vec[BFC1:BFC1 + 1, cols]
            sigma = jax.nn.sigmoid(GELU * pre)
            act = pre * sigma
            ACT[rows, cols] = act.astype(bf16)
            DAC[rows, cols] = (sigma + GELU * act * (1.0 - sigma)).astype(bf16)
        over_columns(UC, 256, body)
        rs_ready(1, i)
        for far in (True, False):
            prow = pair(i, (1 - x) if far else x)
            def body2(cols):
                PART[prow, cols] = dot(ACT[prow, :], W2[:, cols], NN).astype(bf16)
            over_columns(D, TC, body2)
            rs_send(1, i, far)

    sums = {}

    def add(name, value):
        sums[name] = value if name not in sums else sums[name] + value

    def f_final(i, factor):
        final = MID[local(i), :] + rs_finish(1, i) + vrow(BFC2)
        out[local(i), :] = final.astype(bf16)
        difference = final - tea[local(i), :].astype(f32)
        masked = difference * rmask[local(i), 0:1]
        add("loss", jnp.sum(jnp.sum(masked * difference, axis=0, keepdims=True), axis=1, keepdims=True))
        grad_final = masked * factor
        DIF[local(i), :] = grad_final
        add("b_fc2", rowsum(grad_final))
        N3[block(i, own_t), :] = grad_final.astype(bf16)
        ag_start(2, N3, i)

    def b_feed(i):
        rows = pl.ds(i * IR, IR)
        ag_wait(2, i)
        def body(cols):
            grad = dot(N3[rows, :], W2[cols, :], NT) * DAC[rows, cols].astype(f32)
            grad = grad.astype(bf16)
            DAC[rows, cols] = grad
            total = rowsum(grad.astype(f32))
            USUM[0:1, cols] = total if i == 0 else USUM[0:1, cols] + total
        over_columns(UC, 256, body)
        rs_ready(2, i)
        for far in (True, False):
            prow = pair(i, (1 - x) if far else x)
            def body2(cols):
                PART[prow, cols] = dot(DAC[prow, :], W1[cols, :], NT).astype(bf16)
            over_columns(D, TC, body2)
            rs_send(2, i, far)

    def weight_grad(lhs, rhs, result, m, n):
        step = 256
        for a in range(m // step):
            part = dot(lhs[:, a * step:(a + 1) * step], rhs[...], TN)
            result[a * step:(a + 1) * step, :] = part.astype(bf16)

    def b_norm2(i):
        middle = MID[local(i), :]
        _, scaled, inverse = layer_norm(middle, vrow(LN2G), vrow(LN2S))
        upstream = rs_finish(2, i)
        add("ln2g", rowsum(upstream * scaled))
        add("ln2s", rowsum(upstream))
        grad_middle = DIF[local(i), :] + norm_backward(upstream, scaled, inverse, vrow(LN2G))
        DIF[local(i), :] = grad_middle
        add("b_out", rowsum(grad_middle))
        N4[block(i, own_t), :] = grad_middle.astype(bf16)
        ag_start(3, N4, i)

    def b_attention(i):
        rows = pl.ds(i * IR, IR)
        ag_wait(3, i)
        GA[...] = dot(N4[rows, :], Wo[...], NT).astype(bf16)
        grad = GA[...]
        weighed = grad.astype(f32) * ATT[rows, :].astype(f32)
        query_t = QKV[rows, 0:HC].T
        grad_t = grad.T
        acc, keys_t, values_t = None, [], []
        for h in range(HC // HD):
            pick = lane_head == h
            row_dot = jnp.sum(jnp.where(pick, weighed, 0.0), axis=-1, keepdims=True)
            values = jnp.where(pick, QKV[rows, 2 * HC:3 * HC], zero)
            grad_probs = dot(grad, values, NT)
            probs = PR[i * (HC // HD) + h]
            grad_scores = (probs.astype(f32) * ((grad_probs - row_dot) * keep[i:i + 1, :])).astype(bf16)
            keys = jnp.where(pick, QKV[rows, HC:2 * HC], zero)
            part = dot(grad_scores, keys, NN)
            acc = part if acc is None else acc + part
            keys_t.append(dot(query_t[h * HD:(h + 1) * HD, :], grad_scores, NN))
            values_t.append(dot(grad_t[h * HD:(h + 1) * HD, :], probs, NN))
        grad_query = (acc * (HD ** -0.5)).astype(bf16)
        grad_key = jnp.concatenate(keys_t, axis=0).astype(bf16).T
        grad_value = jnp.concatenate(values_t, axis=0).astype(bf16).T
        GP[rows, 0:HC] = grad_query
        GP[rows, HC:2 * HC] = grad_key
        GP[rows, 2 * HC:3 * HC] = grad_value
        add("b_q", rowsum(grad_query.astype(f32)))
        add("b_v", rowsum(grad_value.astype(f32)))
        rs_ready(3, i)
        for far in (True, False):
            prow = pair(i, (1 - x) if far else x)
            def body2(cols):
                PART[prow, cols] = dot(GP[prow, :], Wq[cols, :], NT).astype(bf16)
            over_columns(D, TC, body2)
            rs_send(3, i, far)

    def b_norm1(i):
        _, scaled, inverse = layer_norm(tok[local(i), :].astype(f32), vrow(LN1G), vrow(LN1S))
        upstream = rs_finish(3, i)
        add("ln1g", rowsum(upstream * scaled))
        add("ln1s", rowsum(upstream))
        gtok[local(i), :] = DIF[local(i), :] + norm_backward(upstream, scaled, inverse, vrow(LN1G))

    images = list(range(I))
    weight_send(0)
    counting = count_start()
    for i in images:
        f_norm1(i)
    weight_send(1)
    weight_send(2)
    counting = count_next(counting)
    for i in images:
        ag_forward(0, N1, i)
    weight_forward(0)
    weight_send(3)
    weight_wait(0)
    for i in images:
        ag_wait(0, i)
        if i == 0:
            weight_forward(1)
            weight_wait(1)
        f_attention(i)
        rs_mid(0, i)
    weight_forward(2)
    for i in images:
        f_norm2(i)
    weight_forward(3)
    weight_wait(2)
    weight_wait(3)
    for i in images:
        ag_forward(1, N2, i)
        f_feed(i)
        rs_mid(1, i)
    count = count_end(counting)
    normalizer = count * float(D)
    factor = vec[LSC:LSC + 1, 0:1] * 2.0 / normalizer
    for i in images:
        f_final(i, factor)
    for i in images:
        ag_forward(2, N3, i)
        b_feed(i)
        rs_mid(2, i)
    weight_grad(ACT, N3, GW2, UC, D)
    grad_y(3)
    weight_grad(N2, DAC, GW1, D, UC)
    grad_y(2)
    for i in images:
        b_norm2(i)
    grad_z(3)
    for i in images:
        ag_forward(3, N4, i)
        b_attention(i)
        rs_mid(3, i)
    grad_z(2)
    weight_grad(N1, GP, GWq, D, 3 * HC)
    grad_y(0)
    weight_grad(ATT, N4, GWo, HC, D)
    grad_y(1)

    for n in range(4):
        VE[0, n:n + 1, :] = jnp.where(tensor == n, USUM[0:1, :], 0.0)
    VE[0, 4:5, :] = sums["ln2g"]
    VE[0, 5:6, :] = sums["ln2s"]
    VE[0, 6:7, :] = sums["b_fc2"]
    VE[0, 7:8, :] = sums["b_out"]
    VE[0, 8:9, :] = jnp.broadcast_to(sums["loss"], (1, D))
    VE[0, 9:16, :] = jnp.zeros((7, D), f32)
    vecE[...] = vector_sum(VE, 16)
    vecE[8:9, :] = vecE[8:9, :] / normalizer
    grad_z(0)
    grad_z(1)
    for i in images:
        b_norm1(i)
    VL[0] = jnp.zeros((8, D), f32)
    VL[0, 0:1, :] = sums["ln1g"]
    VL[0, 1:2, :] = sums["ln1s"]
    VL[0, 2:3, aligned(tensor * HC, HC)] = sums["b_q"]
    VL[0, 3:4, aligned(tensor * HC, HC)] = sums["b_v"]
    vecL[...] = vector_sum(VL, 8)
    for w in (3, 2, 0, 1):
        grad_end(w)
    net.finish()


def body(
    mesh_dp, tokens, valid_mask, teacher, loss_scale, ln1_gain, ln1_shift, w_qkv, b_qv, w_out, b_out,
    ln2_gain, ln2_shift, w_fc1, b_fc1, w_fc2, b_fc2,
):
    rows, I, D = tokens.shape
    seq = valid_mask.shape[0]
    parts = seq // rows
    HC, UC = w_qkv.shape[2], w_fc1.shape[1]
    LR = -(-rows // 16) * 16
    IR = parts * LR
    inside = mesh_dp == 8
    part = lax.axis_index("tensor")

    def pad_rows(values):
        values = jnp.transpose(values, (1, 0, 2))
        return jnp.pad(values, ((0, 0), (0, LR - rows), (0, 0))).reshape(I * LR, D)

    tok, tea = pad_rows(tokens), pad_rows(teacher)
    valid = valid_mask.T.astype(f32)
    mine = lax.dynamic_slice_in_dim(valid, part * rows, rows, 1)
    rmask = jnp.pad(mine, ((0, 0), (0, LR - rows))).reshape(I * LR, 1)
    rmask = jnp.broadcast_to(rmask, (I * LR, 128))
    split = valid.reshape(I, parts, rows)
    kept = jnp.pad(split, ((0, 0), (0, 0), (0, LR - rows))).reshape(I, IR)
    bias = jnp.pad(
        jnp.where(split > 0, 0.0, MASKED), ((0, 0), (0, 0), (0, LR - rows)), constant_values=PADDED
    ).reshape(I, IR)
    keep = jnp.concatenate([kept, bias, jnp.zeros((8 - 2 * I, IR), f32)], axis=0)
    pair = lax.dynamic_slice_in_dim(b_qv, part * HC, HC, 1)
    units = lax.dynamic_slice_in_dim(b_fc1, part * UC, UC, 0)
    bias_row = jnp.concatenate([pair[0], jnp.zeros((HC,), f32), pair[1], jnp.zeros((D - 3 * HC,), f32)])
    if inside:
        count = jnp.zeros((), f32)
        weights = (w_qkv.reshape(-1, 3 * HC), w_out, w_fc1, w_fc2)
        gdt = f32
    else:
        count = lax.psum(jnp.sum(valid), "dp")
        weights = (
            lax.all_gather(w_qkv, "dp", axis=0, tiled=True).reshape(-1, 3 * HC),
            lax.all_gather(w_out, "dp", axis=1, tiled=True),
            lax.all_gather(w_fc1, "dp", axis=0, tiled=True),
            lax.all_gather(w_fc2, "dp", axis=1, tiled=True),
        )
        gdt = bf16
    KS = w_fc1.shape[0]
    vec = jnp.stack(
        [ln1_gain, ln1_shift, ln2_gain, ln2_shift, b_out, b_fc2, units, bias_row,
         jnp.broadcast_to(loss_scale, (D,)), jnp.broadcast_to(count, (D,))]
        + [jnp.zeros((D,), f32)] * 6
    )
    size = dict(I=I, LR=LR, IR=IR, D=D, HC=HC, UC=UC, KS=KS, inside=inside)
    H = HC // HD
    VM = pltpu.VMEM
    if inside:
        gshapes = [(KS, 3 * HC), (HC, KS), (KS, UC), (UC, KS)]
    else:
        gshapes = [(D, 3 * HC), (HC, D), (D, UC), (UC, D)]
    k4, k3 = (4, 3) if inside else (1, 1)
    part_shapes = gshapes if inside else [(16, 128)] * 4
    scratch = [
        VM((D, 3 * HC), bf16), VM((HC, D), bf16), VM((D, UC), bf16), VM((UC, D), bf16),
        VM((I * IR, D), bf16), VM((I * IR, D), bf16), VM((I * IR, D), bf16), VM((I * IR, D), bf16),
        VM((I * IR, 3 * HC), bf16), VM((I * H, IR, IR), bf16), VM((I * IR, HC), bf16),
        VM((I * IR, UC), bf16), VM((I * IR, UC), bf16), VM((IR, HC), bf16), VM((I * IR, 3 * HC), bf16),
        VM((I * IR, D), bf16), VM((2 * I * LR, D), bf16), VM((I * LR, D), bf16), VM((I * LR, D), bf16),
        VM((I * LR, D), f32), VM((I * LR, D), f32),
        VM((D, 3 * HC), bf16), VM((HC, D), bf16), VM((D, UC), bf16), VM((UC, D), bf16),
    ]
    scratch += [VM((k4,) + s, bf16) for s in part_shapes]
    scratch += [VM((k3,) + s, bf16) for s in part_shapes]
    scratch += [
        VM((8, UC), f32), VM((10, 16, D), f32), VM((10, 8, D), f32), VM((6, 8, 128), f32),
        pltpu.SemaphoreType.DMA((4,)), pltpu.SemaphoreType.DMA((130,)), pltpu.SemaphoreType.DMA((130,)),
    ]
    vm, hbm = pl.BlockSpec(memory_space=pltpu.VMEM), pl.BlockSpec(memory_space=pl.ANY)
    shape = jax.ShapeDtypeStruct
    results = pl.pallas_call(
        functools.partial(kernel, size),
        out_shape=[shape((I * LR, D), bf16), shape((I * LR, D), f32)]
        + [shape(s, gdt) for s in gshapes]
        + [shape((16, D), f32), shape((8, D), f32)],
        in_specs=[vm] * 5 + [hbm] * 4,
        out_specs=[vm] * 8,
        scratch_shapes=scratch,
        compiler_params=pltpu.CompilerParams(
            collective_id=0, has_side_effects=True, vmem_limit_bytes=64 * 2 ** 20 - 2 ** 16
        ),
    )(tok, tea, rmask, keep, vec, *weights)
    out, gtok, gq, go, g1, g2, early, late = results

    def unpad(values):
        return jnp.transpose(values.reshape(I, LR, D)[:, :rows], (1, 0, 2))

    dp = lax.axis_index("dp")
    index = dp * parts + part
    if not inside:
        gq = lax.psum_scatter(gq, "dp", scatter_dimension=0, tiled=True).astype(f32)
        go = lax.psum_scatter(go, "dp", scatter_dimension=1, tiled=True).astype(f32)
        g1 = lax.psum_scatter(g1, "dp", scatter_dimension=0, tiled=True).astype(f32)
        g2 = lax.psum_scatter(g2, "dp", scatter_dimension=1, tiled=True).astype(f32)
        early, late = lax.psum((early, late), "dp")
    n = D // (mesh_dp * parts)
    early_cut = lax.dynamic_slice_in_dim(early, index * n, n, 1)
    late_cut = lax.dynamic_slice_in_dim(late, index * n, n, 1)
    m = parts * UC // (mesh_dp * parts)
    units_cut = lax.dynamic_slice_in_dim(early[0:parts].reshape(-1), index * m, m, 0)
    return (
        unpad(out),
        early[8, 0],
        unpad(gtok),
        late_cut[0],
        late_cut[1],
        gq.reshape(-1, 3, HC),
        late_cut[2:4],
        go,
        early_cut[7],
        early_cut[4],
        early_cut[5],
        g1,
        units_cut,
        g2,
        early_cut[6],
    )


def solution(mesh):
    in_specs = (
        P("tensor", "dp", None), P(None, "dp"), P("tensor", "dp", None), P(), P(), P(),
        P("dp", None, "tensor"), P(), P("tensor", "dp"), P(), P(), P(), P("dp", "tensor"), P(),
        P("tensor", "dp"), P(),
    )
    both = ("dp", "tensor")
    out_specs = (
        P("tensor", "dp", None), P(), P("tensor", "dp", None), P(both), P(both), P("dp", None, "tensor"),
        P(None, both), P("tensor", "dp"), P(both), P(both), P(both), P("dp", "tensor"), P(both),
        P("tensor", "dp"), P(both),
    )
    return jax.shard_map(
        functools.partial(body, mesh.shape["dp"]), mesh=mesh, in_specs=in_specs, out_specs=out_specs,
        check_vma=False,
    )
```

```python
import functools

import jax
import jax.numpy as jnp
from jax import lax
from jax.experimental import pallas as pl
from jax.experimental.pallas import tpu as pltpu
from jax.sharding import PartitionSpec as P

HD = 64
EPS = 1e-05
MASKED = -1000000000.0
PADDED = -3000000000.0
GELU = 1.702
MESH = pl.DeviceIdType.MESH
f32 = jnp.float32
bf16 = jnp.bfloat16
NN = (((1,), (0,)), ((), ()))
NT = (((1,), (1,)), ((), ()))
TN = (((0,), (0,)), ((), ()))

LN1G, LN1S, LN2G, LN2S, BOUT, BFC2, BFC1, BQKV, LSC, CNT = range(10)


def dot(a, b, dims):
    return lax.dot_general(a, b, dims, preferred_element_type=f32)


def layer_norm(values, gain, shift):
    center = values - jnp.mean(values, axis=-1, keepdims=True)
    inverse = lax.rsqrt(jnp.mean(center * center, axis=-1, keepdims=True) + EPS)
    scaled = center * inverse
    return scaled * gain + shift, scaled, inverse


def norm_backward(upstream, scaled, inverse, gain):
    weighted = upstream * gain
    inner = weighted - jnp.mean(weighted, axis=-1, keepdims=True)
    inner = inner - scaled * jnp.mean(weighted * scaled, axis=-1, keepdims=True)
    return inverse * inner


def rowsum(values):
    return jnp.sum(values, axis=0, keepdims=True)


def aligned(start, size):
    return pl.ds(pl.multiple_of(start, size), size)


class Copies:
    def __init__(self, send, recv):
        self.send, self.recv, self.count = send, recv, 0
        self.all = []

    def make(self, src, dst, device):
        copy = pltpu.make_async_remote_copy(
            src_ref=src,
            dst_ref=dst,
            send_sem=self.send.at[self.count],
            recv_sem=self.recv.at[self.count],
            device_id=device,
            device_id_type=MESH,
        )
        self.count += 1
        return copy

    def start(self, src, dst, device):
        copy = self.make(src, dst, device)
        copy.start()
        self.all.append(copy)
        return copy

    def wait_send(self, copy):
        copy.wait_send()
        self.all = [other for other in self.all if other is not copy]

    def finish(self):
        for copy in self.all:
            copy.wait_send()
        self.all = []


def kernel(
    size,
    tok, tea, rmask, keep, vec, wq, wo, w1, w2,
    out, gtok, gq, go, g1, g2, vecE, vecL,
    Wq, Wo, W1, W2, N1, N2, N3, N4, QKV, PR, ATT, ACT, DAC, GA, GP, PART, RA, RX, XS, MID, DIF,
    GWq, GWo, GW1, GW2, YRq, YRo, YR1, YR2, ZRq, ZRo, ZR1, ZR2,
    USUM, VE, VL, CN, local_sem, send_sem, recv_sem,
):
    I, LR, IR, D, HC, UC = size["I"], size["LR"], size["IR"], size["D"], size["HC"], size["UC"]
    inside = size["inside"]
    KS = size["KS"]
    dp, tensor = lax.axis_index("dp"), lax.axis_index("tensor")
    z, y, x, c = dp // 2, dp % 2, tensor // 2, tensor % 2
    mate = (dp, x * 2 + 1 - c)
    xnei = (dp, (1 - x) * 2 + c)
    ynei = (z * 2 + 1 - y, tensor)

    def zat(k):
        return (z, z + 1 - 2 * (z % 2), lax.rem(z + 2, 4), 3 - z)[k]

    def zdev(k):
        return (zat(k) * 2 + y, tensor)

    net = Copies(send_sem, recv_sem)

    barrier = pltpu.get_barrier_semaphore()
    peers = [mate, xnei] + ([ynei] + [zdev(k) for k in (1, 2, 3)] if inside else [])
    for peer in peers:
        pl.semaphore_signal(barrier, inc=1, device_id=peer, device_id_type=MESH)
    pl.semaphore_wait(barrier, len(peers))

    weights = [(wq, Wq, 0, YRq, ZRq, GWq, gq), (wo, Wo, 1, YRo, ZRo, GWo, go),
               (w1, W1, 0, YR1, ZR1, GW1, g1), (w2, W2, 1, YR2, ZR2, GW2, g2)]

    def shard(ref, axis, index):
        place = pl.ds(pl.multiple_of(index * KS, KS), KS)
        return ref.at[place, :] if axis == 0 else ref.at[:, place]

    gathers = {}
    locals_ = []

    def weight_send(w):
        arg, full, axis = weights[w][:3]
        mine = shard(full, axis, dp) if inside else full
        copy = pltpu.make_async_copy(arg, mine, local_sem.at[w])
        copy.start()
        locals_.append(copy)
        if inside:
            gathers[w] = {k: net.start(arg, mine, zdev(k)) for k in (1, 2, 3)}, []

    def weight_own(w):
        if inside:
            arg, full, axis = weights[w][:3]
            gathers[w][1].append(net.start(arg, shard(full, axis, dp), ynei))

    def weight_forward(w, *ks):
        if not inside:
            return
        full, axis = weights[w][1:3]
        zs, ys = gathers[w]
        for k in ks:
            zs[k].wait_recv()
            got = shard(full, axis, zat(k) * 2 + y)
            ys.append(net.start(got, got, ynei))

    def weight_wait(w):
        locals_[w].wait()
        if inside:
            for copy in gathers[w][1]:
                copy.wait_recv()

    scatters = {w: ({}, {}) for w in range(4)}
    order = (2, 3, 1, 0)

    def weight_grad(w, lhs, rhs):
        axis, YR, GW = weights[w][2], weights[w][3], weights[w][5]
        step = GW.shape[axis] // 4
        for k in order:
            place = aligned(zat(k) * step, step)
            if axis == 0:
                GW[place, :] = dot(lhs[:, place], rhs[...], TN).astype(bf16)
            else:
                GW[:, place] = dot(lhs[...], rhs[:, place], TN).astype(bf16)
            if inside:
                part = shard(GW, axis, zat(k) * 2 + 1 - y)
                scatters[w][0][k] = net.start(part, YR.at[k], ynei)

    def grad_z(w, *ks):
        if not inside:
            return
        axis, YR, ZR, GW = weights[w][2:6]
        for k in ks:
            scatters[w][0][k].wait_recv()
            place = shard(GW, axis, zat(k) * 2 + y)
            place[...] = (place[...].astype(f32) + YR[k].astype(f32)).astype(bf16)
            scatters[w][1][k] = net.start(place, ZR.at[k - 1], zdev(k))

    def grad_end(w):
        axis, YR, ZR, GW, result = weights[w][2:7]
        if not inside:
            result[...] = GW[...]
            return
        scatters[w][0][0].wait_recv()
        total = shard(GW, axis, dp)[...].astype(f32) + YR[0].astype(f32)
        for k in (1, 2, 3):
            scatters[w][1][k].wait_recv()
            total = total + ZR[k - 1].astype(f32)
        result[...] = total

    def vector_sum(V):
        copy = net.start(V.at[0], V.at[1], mate)
        yield
        copy.wait_recv()
        V[2] = V[0] + V[1]
        copy = net.start(V.at[2], V.at[3], xnei)
        yield
        copy.wait_recv()
        if not inside:
            V[10] = V[2] + V[3]
            return
        V[4] = V[2] + V[3]
        copy = net.start(V.at[4], V.at[5], ynei)
        yield
        copy.wait_recv()
        V[6 + z] = V[4] + V[5]
        copies = [net.start(V.at[6 + z], V.at[6 + z], zdev(k)) for k in (1, 2, 3)]
        yield
        for copy in copies:
            copy.wait_recv()
        V[10] = (V[6] + V[7]) + (V[8] + V[9])

    def advance(steps):
        next(steps, None)

    def count_start():
        if not inside:
            return None
        CN[z] = jnp.broadcast_to(jnp.sum(keep[0:I, :], keepdims=True), (8, 128))
        return [net.start(CN.at[z], CN.at[z], zdev(k)) for k in (1, 2, 3)]

    def count_next(copies):
        if not inside:
            return None
        for copy in copies:
            copy.wait_recv()
        CN[4] = (CN[0] + CN[1]) + (CN[2] + CN[3])
        return net.start(CN.at[4], CN.at[5], ynei)

    def count_end(copy):
        if not inside:
            return vec[CNT:CNT + 1, 0:1]
        copy.wait_recv()
        return CN[4, 0:1, 0:1] + CN[5, 0:1, 0:1]

    def block(i, t):
        return aligned((i * 4 + t) * LR, LR)

    def local(i):
        return pl.ds(i * LR, LR)

    def pair(i, xx):
        return aligned(i * IR + xx * 2 * LR, 2 * LR)

    own_t, other_t = tensor, (1 - x) * 2 + c
    ag, rs = {}, {}

    def ag_start(s, N, i):
        mine = N.at[block(i, own_t), :]
        ag[s, i] = [net.start(mine, mine, xnei), net.start(mine, mine, mate)]

    def ag_forward(s, N, i):
        ag[s, i][0].wait_recv()
        got = N.at[block(i, other_t), :]
        ag[s, i].append(net.start(got, got, mate))

    def ag_wait(s, i):
        ag[s, i][1].wait_recv()
        ag[s, i][2].wait_recv()

    def landing(ref, n):
        return ref.at[pl.ds(n * LR, LR), :]

    def rs_ready(s, i):
        if s:
            for copy in rs[s - 1, i][:2]:
                net.wait_send(copy)

    def rs_send(s, i, far):
        base = i * IR + ((1 - x) if far else x) * 2 * LR
        src = PART.at[aligned(base + (1 - c) * LR, LR), :]
        rs.setdefault((s, i), []).append(net.start(src, landing(RA, i * 2 + (0 if far else 1)), mate))

    def rs_mid(s, i):
        rs[s, i][0].wait_recv()
        if s:
            net.wait_send(rs[s - 1, i][2])
        kept = PART[aligned(i * IR + (1 - x) * 2 * LR + c * LR, LR), :]
        XS[local(i), :] = (kept.astype(f32) + landing(RA, i * 2)[...].astype(f32)).astype(bf16)
        rs[s, i].append(net.start(XS.at[local(i), :], landing(RX, i), xnei))

    def rs_finish(s, i):
        rs[s, i][1].wait_recv()
        rs[s, i][2].wait_recv()
        kept = PART[aligned(i * IR + x * 2 * LR + c * LR, LR), :].astype(f32)
        return kept + landing(RA, i * 2 + 1)[...].astype(f32) + landing(RX, i)[...].astype(f32)

    def vrow(n, lo=0, hi=None):
        return vec[n:n + 1, lo:(D if hi is None else hi)]

    TC = 512 if D % 512 == 0 and UC % 512 == 0 else 256

    def over_columns(n, step, body):
        for j in range(n // step):
            body(pl.ds(j * step, step))

    def f_norm1(i):
        normed = layer_norm(tok[local(i), :].astype(f32), vrow(LN1G), vrow(LN1S))[0]
        N1[block(i, own_t), :] = normed.astype(bf16)
        ag_start(0, N1, i)

    lane_head = lax.broadcasted_iota(jnp.int32, (1, HC), 1) // HD
    zero = jnp.zeros((), bf16)

    def f_attention(i, before_heads, before_out):
        rows = pl.ds(i * IR, IR)
        for n in range(3):
            def body(cols):
                proj = dot(N1[rows, :], Wq[:, cols], NN) + vec[BQKV:BQKV + 1, cols]
                if n == 0:
                    proj = proj.astype(bf16).astype(f32) * (HD ** -0.5)
                QKV[rows, cols] = proj.astype(bf16)
            body(pl.ds(n * HC, HC))
        before_heads()
        acc = None
        for h in range(HC // HD):
            pick = lane_head == h
            keys = jnp.where(pick, QKV[rows, HC:2 * HC], zero)
            scores = dot(QKV[rows, 0:HC], keys, NT)
            scores = scores * keep[i:i + 1, :] + keep[I + i:I + i + 1, :]
            expo = jnp.exp(scores - jnp.max(scores, axis=-1, keepdims=True))
            probs = (expo * (1.0 / jnp.sum(expo, axis=-1, keepdims=True))).astype(bf16)
            PR[i * (HC // HD) + h] = probs
            values = jnp.where(pick, QKV[rows, 2 * HC:3 * HC], zero)
            part = dot(probs, values, NN)
            acc = part if acc is None else acc + part
        ATT[rows, :] = acc.astype(bf16)
        before_out()
        rs_ready(0, i)
        for far in (True, False):
            prow = pair(i, (1 - x) if far else x)
            def body(cols):
                PART[prow, cols] = dot(ATT[prow, :], Wo[:, cols], NN).astype(bf16)
            over_columns(D, TC, body)
            rs_send(0, i, far)

    def f_norm2(i):
        middle = tok[local(i), :].astype(f32) + rs_finish(0, i) + vrow(BOUT)
        MID[local(i), :] = middle
        N2[block(i, own_t), :] = layer_norm(middle, vrow(LN2G), vrow(LN2S))[0].astype(bf16)
        ag_start(1, N2, i)

    def f_feed(i):
        rows = pl.ds(i * IR, IR)
        ag_wait(1, i)
        def body(cols):
            pre = dot(N2[rows, :], W1[:, cols], NN) + vec[BFC1:BFC1 + 1, cols]
            sigma = jax.nn.sigmoid(GELU * pre)
            act = pre * sigma
            ACT[rows, cols] = act.astype(bf16)
            DAC[rows, cols] = (sigma + GELU * act * (1.0 - sigma)).astype(bf16)
        over_columns(UC, 256, body)

    def f_feed_out(i):
        rs_ready(1, i)
        for far in (True, False):
            prow = pair(i, (1 - x) if far else x)
            def body2(cols):
                PART[prow, cols] = dot(ACT[prow, :], W2[:, cols], NN).astype(bf16)
            over_columns(D, TC, body2)
            rs_send(1, i, far)

    sums = {}

    def add(name, value):
        sums[name] = value if name not in sums else sums[name] + value

    def f_final(i, factor):
        final = MID[local(i), :] + rs_finish(1, i) + vrow(BFC2)
        out[local(i), :] = final.astype(bf16)
        difference = final - tea[local(i), :].astype(f32)
        masked = difference * rmask[local(i), 0:1]
        add("loss", jnp.sum(jnp.sum(masked * difference, axis=0, keepdims=True), axis=1, keepdims=True))
        grad_final = masked * factor
        DIF[local(i), :] = grad_final
        add("b_fc2", rowsum(grad_final))
        N3[block(i, own_t), :] = grad_final.astype(bf16)
        ag_start(2, N3, i)

    def b_feed(i):
        rows = pl.ds(i * IR, IR)
        def body(cols):
            grad = dot(N3[rows, :], W2[cols, :], NT) * DAC[rows, cols].astype(f32)
            grad = grad.astype(bf16)
            DAC[rows, cols] = grad
            total = rowsum(grad.astype(f32))
            USUM[0:1, cols] = total if i == 0 else USUM[0:1, cols] + total
        over_columns(UC, 256, body)
        rs_ready(2, i)
        for far in (True, False):
            prow = pair(i, (1 - x) if far else x)
            def body2(cols):
                PART[prow, cols] = dot(DAC[prow, :], W1[cols, :], NT).astype(bf16)
            over_columns(D, TC, body2)
            rs_send(2, i, far)

    def b_norm2(i):
        middle = MID[local(i), :]
        _, scaled, inverse = layer_norm(middle, vrow(LN2G), vrow(LN2S))
        upstream = rs_finish(2, i)
        add("ln2g", rowsum(upstream * scaled))
        add("ln2s", rowsum(upstream))
        grad_middle = DIF[local(i), :] + norm_backward(upstream, scaled, inverse, vrow(LN2G))
        DIF[local(i), :] = grad_middle
        add("b_out", rowsum(grad_middle))
        N4[block(i, own_t), :] = grad_middle.astype(bf16)
        ag_start(3, N4, i)

    def b_attention(i):
        rows = pl.ds(i * IR, IR)
        GA[...] = dot(N4[rows, :], Wo[...], NT).astype(bf16)
        grad = GA[...]
        weighed = grad.astype(f32) * ATT[rows, :].astype(f32)
        query_t = QKV[rows, 0:HC].T
        grad_t = grad.T
        acc, keys_t, values_t = None, [], []
        for h in range(HC // HD):
            pick = lane_head == h
            row_dot = jnp.sum(jnp.where(pick, weighed, 0.0), axis=-1, keepdims=True)
            values = jnp.where(pick, QKV[rows, 2 * HC:3 * HC], zero)
            grad_probs = dot(grad, values, NT)
            probs = PR[i * (HC // HD) + h]
            grad_scores = (probs.astype(f32) * ((grad_probs - row_dot) * keep[i:i + 1, :])).astype(bf16)
            keys = jnp.where(pick, QKV[rows, HC:2 * HC], zero)
            part = dot(grad_scores, keys, NN)
            acc = part if acc is None else acc + part
            keys_t.append(dot(query_t[h * HD:(h + 1) * HD, :], grad_scores, NN))
            values_t.append(dot(grad_t[h * HD:(h + 1) * HD, :], probs, NN))
        grad_query = (acc * (HD ** -0.5)).astype(bf16)
        grad_key = jnp.concatenate(keys_t, axis=0).astype(bf16).T
        grad_value = jnp.concatenate(values_t, axis=0).astype(bf16).T
        GP[rows, 0:HC] = grad_query
        GP[rows, HC:2 * HC] = grad_key
        GP[rows, 2 * HC:3 * HC] = grad_value
        add("b_q", rowsum(grad_query.astype(f32)))
        add("b_v", rowsum(grad_value.astype(f32)))
        rs_ready(3, i)
        for far in (True, False):
            prow = pair(i, (1 - x) if far else x)
            def body2(cols):
                PART[prow, cols] = dot(GP[prow, :], Wq[cols, :], NT).astype(bf16)
            over_columns(D, TC, body2)
            rs_send(3, i, far)

    def b_norm1(i):
        _, scaled, inverse = layer_norm(tok[local(i), :].astype(f32), vrow(LN1G), vrow(LN1S))
        upstream = rs_finish(3, i)
        add("ln1g", rowsum(upstream * scaled))
        add("ln1s", rowsum(upstream))
        gtok[local(i), :] = DIF[local(i), :] + norm_backward(upstream, scaled, inverse, vrow(LN1G))

    def nothing():
        pass

    images = list(range(I))
    first, last = images[0], images[-1]
    weight_send(0)
    weight_own(0)
    counting = count_start()
    for i in images:
        f_norm1(i)
    weight_forward(0, 1)
    ag_forward(0, N1, first)
    weight_forward(0, 2)
    for i in images[1:]:
        ag_forward(0, N1, i)
    weight_forward(0, 3)
    counting = count_next(counting)
    weight_wait(0)
    weight_send(1)
    weight_own(1)
    weight_send(2)
    weight_send(3)

    def out_forward():
        weight_forward(1, 1, 2, 3)
        weight_own(2)
        weight_own(3)

    for i in images:
        ag_wait(0, i)
        if i == first:
            f_attention(i, out_forward, lambda: weight_wait(1))
        else:
            f_attention(i, nothing, nothing)
        rs_mid(0, i)
        if i == first:
            weight_forward(2, 1)
    weight_forward(2, 2)
    f_norm2(first)
    weight_forward(2, 3)
    for i in images[1:]:
        f_norm2(i)
    ag_forward(1, N2, first)
    weight_forward(3, 1)
    weight_wait(2)
    f_feed(first)
    weight_forward(3, 2)
    for i in images[1:]:
        ag_forward(1, N2, i)
        f_feed(i)
    weight_forward(3, 3)
    weight_wait(3)
    for i in images:
        f_feed_out(i)
        rs_mid(1, i)
    count = count_end(counting)
    normalizer = count * float(D)
    factor = vec[LSC:LSC + 1, 0:1] * 2.0 / normalizer
    for i in images:
        f_final(i, factor)
    for i in images:
        ag_forward(2, N3, i)
        ag_wait(2, i)
        if i == last:
            weight_grad(3, ACT, N3)
        b_feed(i)
        rs_mid(2, i)
    weight_grad(2, N2, DAC)
    grad_z(3, 2)
    b_norm2(first)
    grad_z(3, 3)
    for i in images[1:]:
        b_norm2(i)
    grad_z(3, 1)
    for i in images:
        ag_forward(3, N4, i)
        ag_wait(3, i)
        if i == last:
            weight_grad(1, ATT, N4)
        b_attention(i)
        rs_mid(3, i)
        if i == first:
            grad_z(2, 2, 3)
    weight_grad(0, N1, GP)
    grad_z(2, 1)
    grad_z(1, 2, 3, 1)

    for n in range(4):
        VE[0, n:n + 1, :] = jnp.where(tensor == n, USUM[0:1, :], 0.0)
    VE[0, 4:5, :] = sums["ln2g"]
    VE[0, 5:6, :] = sums["ln2s"]
    VE[0, 6:7, :] = sums["b_fc2"]
    VE[0, 7:8, :] = sums["b_out"]
    VE[0, 8:9, :] = jnp.broadcast_to(sums["loss"], (1, D))
    VE[0, 9:16, :] = jnp.zeros((7, D), f32)
    early = vector_sum(VE)
    advance(early)
    grad_z(0, 2)
    b_norm1(first)
    advance(early)
    grad_z(0, 3)
    for i in images[1:]:
        b_norm1(i)
    VL[0] = jnp.zeros((8, D), f32)
    VL[0, 0:1, :] = sums["ln1g"]
    VL[0, 1:2, :] = sums["ln1s"]
    VL[0, 2:3, aligned(tensor * HC, HC)] = sums["b_q"]
    VL[0, 3:4, aligned(tensor * HC, HC)] = sums["b_v"]
    late = vector_sum(VL)
    advance(late)
    grad_z(0, 1)
    advance(early)
    advance(late)
    advance(early)
    grad_end(3)
    advance(late)
    grad_end(2)
    advance(late)
    grad_end(1)
    advance(early)
    vecE[...] = VE[10]
    vecE[8:9, :] = VE[10, 8:9, :] / normalizer
    grad_end(0)
    advance(late)
    vecL[...] = VL[10]
    net.finish()


def body(
    mesh_dp, tokens, valid_mask, teacher, loss_scale, ln1_gain, ln1_shift, w_qkv, b_qv, w_out, b_out,
    ln2_gain, ln2_shift, w_fc1, b_fc1, w_fc2, b_fc2,
):
    rows, I, D = tokens.shape
    seq = valid_mask.shape[0]
    parts = seq // rows
    HC, UC = w_qkv.shape[2], w_fc1.shape[1]
    LR = -(-rows // 16) * 16
    IR = parts * LR
    inside = mesh_dp == 8
    part = lax.axis_index("tensor")

    def pad_rows(values):
        values = jnp.transpose(values, (1, 0, 2))
        return jnp.pad(values, ((0, 0), (0, LR - rows), (0, 0))).reshape(I * LR, D)

    tok, tea = pad_rows(tokens), pad_rows(teacher)
    valid = valid_mask.T.astype(f32)
    mine = lax.dynamic_slice_in_dim(valid, part * rows, rows, 1)
    rmask = jnp.pad(mine, ((0, 0), (0, LR - rows))).reshape(I * LR, 1)
    rmask = jnp.broadcast_to(rmask, (I * LR, 128))
    split = valid.reshape(I, parts, rows)
    kept = jnp.pad(split, ((0, 0), (0, 0), (0, LR - rows))).reshape(I, IR)
    bias = jnp.pad(
        jnp.where(split > 0, 0.0, MASKED), ((0, 0), (0, 0), (0, LR - rows)), constant_values=PADDED
    ).reshape(I, IR)
    keep = jnp.concatenate([kept, bias, jnp.zeros((8 - 2 * I, IR), f32)], axis=0)
    pair = lax.dynamic_slice_in_dim(b_qv, part * HC, HC, 1)
    units = lax.dynamic_slice_in_dim(b_fc1, part * UC, UC, 0)
    bias_row = jnp.concatenate([pair[0], jnp.zeros((HC,), f32), pair[1], jnp.zeros((D - 3 * HC,), f32)])
    if inside:
        count = jnp.zeros((), f32)
        weights = (w_qkv.reshape(-1, 3 * HC), w_out, w_fc1, w_fc2)
        gdt = f32
    else:
        count = lax.psum(jnp.sum(valid), "dp")
        weights = (
            lax.all_gather(w_qkv, "dp", axis=0, tiled=True).reshape(-1, 3 * HC),
            lax.all_gather(w_out, "dp", axis=1, tiled=True),
            lax.all_gather(w_fc1, "dp", axis=0, tiled=True),
            lax.all_gather(w_fc2, "dp", axis=1, tiled=True),
        )
        gdt = bf16
    KS = w_fc1.shape[0]
    vec = jnp.stack(
        [ln1_gain, ln1_shift, ln2_gain, ln2_shift, b_out, b_fc2, units, bias_row,
         jnp.broadcast_to(loss_scale, (D,)), jnp.broadcast_to(count, (D,))]
        + [jnp.zeros((D,), f32)] * 6
    )
    size = dict(I=I, LR=LR, IR=IR, D=D, HC=HC, UC=UC, KS=KS, inside=inside)
    H = HC // HD
    VM = pltpu.VMEM
    if inside:
        gshapes = [(KS, 3 * HC), (HC, KS), (KS, UC), (UC, KS)]
    else:
        gshapes = [(D, 3 * HC), (HC, D), (D, UC), (UC, D)]
    k4, k3 = (4, 3) if inside else (1, 1)
    part_shapes = gshapes if inside else [(16, 128)] * 4
    scratch = [
        VM((D, 3 * HC), bf16), VM((HC, D), bf16), VM((D, UC), bf16), VM((UC, D), bf16),
        VM((I * IR, D), bf16), VM((I * IR, D), bf16), VM((I * IR, D), bf16), VM((I * IR, D), bf16),
        VM((I * IR, 3 * HC), bf16), VM((I * H, IR, IR), bf16), VM((I * IR, HC), bf16),
        VM((I * IR, UC), bf16), VM((I * IR, UC), bf16), VM((IR, HC), bf16), VM((I * IR, 3 * HC), bf16),
        VM((I * IR, D), bf16), VM((2 * I * LR, D), bf16), VM((I * LR, D), bf16), VM((I * LR, D), bf16),
        VM((I * LR, D), f32), VM((I * LR, D), f32),
        VM((D, 3 * HC), bf16), VM((HC, D), bf16), VM((D, UC), bf16), VM((UC, D), bf16),
    ]
    scratch += [VM((k4,) + s, bf16) for s in part_shapes]
    scratch += [VM((k3,) + s, bf16) for s in part_shapes]
    scratch += [
        VM((8, UC), f32), VM((11, 16, D), f32), VM((11, 8, D), f32), VM((6, 8, 128), f32),
        pltpu.SemaphoreType.DMA((4,)), pltpu.SemaphoreType.DMA((130,)), pltpu.SemaphoreType.DMA((130,)),
    ]
    vm, hbm = pl.BlockSpec(memory_space=pltpu.VMEM), pl.BlockSpec(memory_space=pl.ANY)
    shape = jax.ShapeDtypeStruct
    results = pl.pallas_call(
        functools.partial(kernel, size),
        out_shape=[shape((I * LR, D), bf16), shape((I * LR, D), f32)]
        + [shape(s, gdt) for s in gshapes]
        + [shape((16, D), f32), shape((8, D), f32)],
        in_specs=[vm] * 5 + [hbm] * 4,
        out_specs=[vm] * 8,
        scratch_shapes=scratch,
        compiler_params=pltpu.CompilerParams(
            collective_id=0, has_side_effects=True, vmem_limit_bytes=64 * 2 ** 20 - 2 ** 16
        ),
    )(tok, tea, rmask, keep, vec, *weights)
    out, gtok, gq, go, g1, g2, early, late = results

    def unpad(values):
        return jnp.transpose(values.reshape(I, LR, D)[:, :rows], (1, 0, 2))

    dp = lax.axis_index("dp")
    index = dp * parts + part
    if not inside:
        gq = lax.psum_scatter(gq, "dp", scatter_dimension=0, tiled=True).astype(f32)
        go = lax.psum_scatter(go, "dp", scatter_dimension=1, tiled=True).astype(f32)
        g1 = lax.psum_scatter(g1, "dp", scatter_dimension=0, tiled=True).astype(f32)
        g2 = lax.psum_scatter(g2, "dp", scatter_dimension=1, tiled=True).astype(f32)
        early, late = lax.psum((early, late), "dp")
    n = D // (mesh_dp * parts)
    early_cut = lax.dynamic_slice_in_dim(early, index * n, n, 1)
    late_cut = lax.dynamic_slice_in_dim(late, index * n, n, 1)
    m = parts * UC // (mesh_dp * parts)
    units_cut = lax.dynamic_slice_in_dim(early[0:parts].reshape(-1), index * m, m, 0)
    return (
        unpad(out),
        early[8, 0],
        unpad(gtok),
        late_cut[0],
        late_cut[1],
        gq.reshape(-1, 3, HC),
        late_cut[2:4],
        go,
        early_cut[7],
        early_cut[4],
        early_cut[5],
        g1,
        units_cut,
        g2,
        early_cut[6],
    )


def solution(mesh):
    in_specs = (
        P("tensor", "dp", None), P(None, "dp"), P("tensor", "dp", None), P(), P(), P(),
        P("dp", None, "tensor"), P(), P("tensor", "dp"), P(), P(), P(), P("dp", "tensor"), P(),
        P("tensor", "dp"), P(),
    )
    both = ("dp", "tensor")
    out_specs = (
        P("tensor", "dp", None), P(), P("tensor", "dp", None), P(both), P(both), P("dp", None, "tensor"),
        P(None, both), P("tensor", "dp"), P(both), P(both), P(both), P("dp", "tensor"), P(both),
        P("tensor", "dp"), P(both),
    )
    return jax.shard_map(
        functools.partial(body, mesh.shape["dp"]), mesh=mesh, in_specs=in_specs, out_specs=out_specs,
        check_vma=False,
    )
```

```python
import functools

import jax
import jax.numpy as jnp
from jax import lax
from jax.experimental import pallas as pl
from jax.experimental.pallas import tpu as pltpu
from jax.sharding import PartitionSpec as P

HD = 64
EPS = 1e-05
MASKED = -1000000000.0
PADDED = -3000000000.0
GELU = 1.702
MESH = pl.DeviceIdType.MESH
f32 = jnp.float32
bf16 = jnp.bfloat16
NN = (((1,), (0,)), ((), ()))
NT = (((1,), (1,)), ((), ()))
TN = (((0,), (0,)), ((), ()))

def dot(a, b, dims):
    return lax.dot_general(a, b, dims, preferred_element_type=f32)


def layer_norm(values, gain, shift):
    center = values - jnp.mean(values, axis=-1, keepdims=True)
    inverse = lax.rsqrt(jnp.mean(center * center, axis=-1, keepdims=True) + EPS)
    scaled = center * inverse
    return scaled * gain + shift, scaled, inverse


def norm_backward(upstream, scaled, inverse, gain):
    weighted = upstream * gain
    inner = weighted - jnp.mean(weighted, axis=-1, keepdims=True)
    inner = inner - scaled * jnp.mean(weighted * scaled, axis=-1, keepdims=True)
    return inverse * inner


def rowsum(values):
    return jnp.sum(values, axis=0, keepdims=True)


def aligned(start, size):
    if isinstance(start, int):
        return pl.ds(start, size)
    return pl.ds(pl.multiple_of(start, size), size)


class Copies:
    def __init__(self, send, recv):
        self.send, self.recv, self.count = send, recv, 0
        self.all = []

    def make(self, src, dst, device):
        copy = pltpu.make_async_remote_copy(
            src_ref=src,
            dst_ref=dst,
            send_sem=self.send.at[self.count],
            recv_sem=self.recv.at[self.count],
            device_id=device,
            device_id_type=MESH,
        )
        self.count += 1
        return copy

    def start(self, src, dst, device):
        copy = self.make(src, dst, device)
        copy.start()
        self.all.append(copy)
        return copy

    def wait_send(self, copy):
        copy.wait_send()
        self.all = [other for other in self.all if other is not copy]

    def finish(self):
        for copy in self.all:
            copy.wait_send()
        self.all = []


def kernel(
    size,
    tok, tea, mask, ln1g, ln1s, ln2g, ln2s, bout, bfc2, bfc1, bqv, lscale, given, wq, wo, w1, w2,
    out, gtok, gq, go, g1, g2, small,
    Wq, Wo, W1, W2, N1, N2, N3, N4, QKV, PR, ATT, ACT, DAC, GA, GP, PART, RA, RX, XS, MID, DIF,
    GWq, GWo, GW1, GW2, YRq, YRo, YR1, YR2, ZRq, ZRo, ZR1, ZR2,
    TOK, KEEP, RM, USUM, VTE, VSE, VPE, VDE, VTL, VSL, VPL, VDL, CN, local_sem, send_sem, recv_sem,
):
    I, LR, IR, D, HC, UC = size["I"], size["LR"], size["IR"], size["D"], size["HC"], size["UC"]
    inside = size["inside"]
    KS, SR = size["KS"], size["SR"]
    dp, tensor = lax.axis_index("dp"), lax.axis_index("tensor")
    z, y, x, c = dp // 2, dp % 2, tensor // 2, tensor % 2
    mate = (dp, x * 2 + 1 - c)
    xnei = (dp, (1 - x) * 2 + c)
    diag = (dp, (1 - x) * 2 + 1 - c)
    ynei = (z * 2 + 1 - y, tensor)

    def zat(k):
        return (z, z + 1 - 2 * (z % 2), lax.rem(z + 2, 4), 3 - z)[k]

    def zdev(k):
        return (zat(k) * 2 + y, tensor)

    net = Copies(send_sem, recv_sem)

    barrier = pltpu.get_barrier_semaphore()
    group = [zat(k) * 2 + y for k in (1, 2, 3)] + [zat(k) * 2 + 1 - y for k in (0, 1, 2, 3)]
    peers = [mate, xnei, diag] + ([(other, tensor) for other in group] if inside else [])
    for peer in peers:
        pl.semaphore_signal(barrier, inc=1, device_id=peer, device_id_type=MESH)
    pl.semaphore_wait(barrier, len(peers))

    weights = [(wq, Wq, 0, YRq, ZRq, GWq, gq), (wo, Wo, 1, YRo, ZRo, GWo, go),
               (w1, W1, 2, YR1, ZR1, GW1, g1), (w2, W2, 1, YR2, ZR2, GW2, g2)]

    def shard(ref, kind, index):
        if kind == 1:
            return ref.at[index]
        place = pl.ds(pl.multiple_of(index * KS, KS), KS)
        return ref.at[:, place, :] if kind == 0 else ref.at[place, :]

    def columns(ref, start, count, rows=slice(None)):
        return jnp.concatenate([ref[n, rows, :] for n in range(start // 128, (start + count) // 128)], axis=1)

    gathers = {}
    locals_ = []

    def weight_send(w):
        arg, full, axis = weights[w][:3]
        mine = shard(full, axis, dp) if inside else full
        copy = pltpu.make_async_copy(arg, mine, local_sem.at[w])
        copy.start()
        locals_.append(copy)
        if inside:
            gathers[w] = {k: net.start(arg, mine, zdev(k)) for k in (1, 2, 3)}, {}

    def weight_own(w):
        if inside:
            arg, full, axis = weights[w][:3]
            gathers[w][1][0] = net.start(arg, shard(full, axis, dp), ynei)

    def weight_forward(w, *ks):
        if not inside:
            return
        full, axis = weights[w][1:3]
        zs, ys = gathers[w]
        for k in ks:
            zs[k].wait_recv()
            got = shard(full, axis, zat(k) * 2 + y)
            ys[k] = net.start(got, got, ynei)

    def weight_wait(w, *ks):
        ks = ks or (0, 1, 2, 3)
        if 0 in ks:
            locals_[w].wait()
        if inside:
            for k in ks:
                gathers[w][1][k].wait_recv()

    scatters = {w: ({}, {}) for w in range(4)}
    order = (3, 1, 2, 0)

    def weight_grad(w, lhs, rhs):
        axis, YR, GW = weights[w][2], weights[w][3], weights[w][5]
        step = D // 4
        for k in order:
            group = zat(k) if inside else k
            place = aligned(group * step, step)
            if w == 0:
                part = dot(lhs[:, place], rhs[...], TN).astype(bf16)
                for n in range(3):
                    GW[n, place, :] = part[:, n * HC:(n + 1) * HC]
            elif w == 2:
                GW[place, :] = dot(lhs[:, place], rhs[...], TN).astype(bf16)
            else:
                part = dot(lhs[...], rhs[:, place], TN).astype(bf16)
                GW[group * 2] = part[:, :128]
                GW[group * 2 + 1] = part[:, 128:]
            if inside:
                scatters[w][0][k] = net.start(shard(GW, axis, group * 2 + 1 - y), YR.at[k], ynei)

    def grad_a(w, *ks):
        if not inside:
            return
        axis, YR, ZR, GW = weights[w][2:6]
        for k in ks:
            scatters[w][0][k].wait_recv()
            place = shard(GW, axis, zat(k) * 2 + y)
            place[...] = (place[...].astype(f32) + YR[k].astype(f32)).astype(bf16)
            scatters[w][1][k] = net.start(place, ZR.at[k // 2], zdev(1))

    def grad_b(w):
        if not inside:
            return
        axis, YR, ZR, GW = weights[w][2:6]
        scatters[w][0][2].wait_recv()
        scatters[w][1][3].wait_recv()
        place = shard(GW, axis, zat(2) * 2 + y)
        total = place[...].astype(f32) + YR[2].astype(f32) + ZR[1].astype(f32)
        place[...] = total.astype(bf16)
        scatters[w][1][2] = net.start(place, ZR.at[2], zdev(2))

    def grad_end(w):
        axis, YR, ZR, GW, result = weights[w][2:7]
        if not inside:
            result[...] = GW[...]
            return
        scatters[w][0][0].wait_recv()
        scatters[w][1][1].wait_recv()
        scatters[w][1][2].wait_recv()
        total = shard(GW, axis, dp)[...].astype(f32) + YR[0].astype(f32)
        result[...] = total + ZR[0].astype(f32) + ZR[2].astype(f32)

    def vector_sum(VT, VS, VP, VD, units):
        copies = [net.start(VT.at[tensor], VT.at[tensor], peer) for peer in (mate, xnei, diag)]
        yield
        for copy in copies:
            copy.wait_recv()
        VS[...] = (VT[0] + VT[1]) + (VT[2] + VT[3])
        if not inside:
            return
        for d in range(8):
            VP[d] = VS[:, d * 128:(d + 1) * 128]
            if units:
                VP[d, 0:1, :] = VS[d // 2:d // 2 + 1, aligned((d % 2 * 4 + tensor) * 128, 128)]
        VD[dp] = VP[dp]
        copies = [net.start(VP.at[other], VD.at[dp], (other, tensor)) for other in group]
        yield
        for copy in copies:
            copy.wait_recv()
        VD[8] = ((VD[0] + VD[1]) + (VD[2] + VD[3])) + ((VD[4] + VD[5]) + (VD[6] + VD[7]))

    def advance(steps):
        next(steps, None)

    def count_start():
        if not inside:
            return None
        CN[z] = jnp.broadcast_to(jnp.sum(mask[...].astype(f32), keepdims=True), (8, 128))
        return [net.start(CN.at[z], CN.at[z], zdev(k)) for k in (1, 2, 3)]

    def count_next(copies):
        if not inside:
            return None
        for copy in copies:
            copy.wait_recv()
        CN[4] = (CN[0] + CN[1]) + (CN[2] + CN[3])
        return net.start(CN.at[4], CN.at[5], ynei)

    def count_end(copy):
        if not inside:
            return given[...]
        copy.wait_recv()
        return CN[4, 0:1, 0:1] + CN[5, 0:1, 0:1]

    def block(i, t):
        return aligned((i * 4 + t) * LR, LR)

    def local(i):
        return pl.ds(i * LR, LR)

    def pair(i, xx):
        return aligned(i * IR + xx * 2 * LR, 2 * LR)

    own_t, other_t = tensor, (1 - x) * 2 + c
    ag, rs = {}, {}

    def ag_start(s, N, i):
        mine = N.at[block(i, own_t), :]
        ag[s, i] = [net.start(mine, mine, xnei), net.start(mine, mine, mate)]

    def ag_forward(s, N, i):
        ag[s, i][0].wait_recv()
        got = N.at[block(i, other_t), :]
        ag[s, i].append(net.start(got, got, mate))

    def ag_wait(s, i):
        ag[s, i][1].wait_recv()
        ag[s, i][2].wait_recv()

    def landing(ref, n):
        return ref.at[pl.ds(n * LR, LR), :]

    half = (z // 2) if inside else 0
    early_cols, late_cols = aligned(half * (D // 2), D // 2), aligned((1 - half) * (D // 2), D // 2)
    all_cols = pl.ds(0, D)

    def rs_ready(s, i):
        for copies in rs.get((s - 1, i), []):
            for copy in copies[:2]:
                net.wait_send(copy)

    def rs_send(s, i, far, cols=all_cols):
        base = i * IR + ((1 - x) if far else x) * 2 * LR
        src = PART.at[aligned(base + (1 - c) * LR, LR), cols]
        dst = RA.at[pl.ds((i * 2 + (0 if far else 1)) * LR, LR), cols]
        if far:
            rs.setdefault((s, i), []).append([])
        rs[s, i][-1].append(net.start(src, dst, mate))

    def rs_mid(s, i, cols=all_cols):
        copies = rs[s, i][-1]
        copies[0].wait_recv()
        if len(rs[s, i]) == 1:
            for before in rs.get((s - 1, i), []):
                net.wait_send(before[2])
        kept = PART[aligned(i * IR + (1 - x) * 2 * LR + c * LR, LR), cols]
        got = RA[pl.ds(i * 2 * LR, LR), cols]
        XS[local(i), cols] = (kept.astype(f32) + got.astype(f32)).astype(bf16)
        copies.append(net.start(XS.at[local(i), cols], RX.at[local(i), cols], xnei))

    def rs_finish(s, i):
        for copies in rs[s, i]:
            copies[1].wait_recv()
            copies[2].wait_recv()
        kept = PART[aligned(i * IR + x * 2 * LR + c * LR, LR), :].astype(f32)
        return kept + landing(RA, i * 2 + 1)[...].astype(f32) + RX[local(i), :].astype(f32)

    def prepare_teacher(i):
        start = (i * 4 + own_t) * LR
        N3[aligned(start + SR // 16 * 16, 16), :] = jnp.zeros((16, D), bf16)
        N3[pl.ds(pl.multiple_of(start, LR), SR), :] = tea[:, i, :]

    def prepare_masks():
        KEEP[...] = jnp.zeros(KEEP.shape, f32)
        for t in range(4):
            KEEP[0:I, t * LR:t * LR + SR] = mask[:, t * SR:(t + 1) * SR].astype(f32)
        near = lax.broadcasted_iota(jnp.int32, (LR, LR), 0) == lax.broadcasted_iota(jnp.int32, (LR, LR), 1)
        for i in range(I):
            row = jnp.zeros((1, LR), f32)
            for t in range(4):
                row = jnp.where(tensor == t, KEEP[i:i + 1, t * LR:(t + 1) * LR], row)
            RM[local(i), 0:1] = jnp.sum(jnp.where(near, row, 0.0), axis=1, keepdims=True)

    TC = 512 if D % 512 == 0 and UC % 512 == 0 else 256

    def over_columns(n, step, body):
        for j in range(n // step):
            body(pl.ds(j * step, step))

    def f_norm1(i):
        TOK[i * LR + SR // 16 * 16:(i + 1) * LR, :] = jnp.zeros((LR - SR // 16 * 16, D), bf16)
        TOK[i * LR:i * LR + SR, :] = tok[:, i, :]
        normed = layer_norm(TOK[local(i), :].astype(f32), ln1g[...], ln1s[...])[0]
        N1[block(i, own_t), :] = normed.astype(bf16)
        ag_start(0, N1, i)

    lane_head = lax.broadcasted_iota(jnp.int32, (1, HC), 1) // HD
    zero = jnp.zeros((), bf16)

    def f_attention(i, before_heads, before_out):
        rows = pl.ds(i * IR, IR)
        place = aligned(tensor * HC, HC)
        for n in range(3):
            proj = dot(N1[rows, :], Wq[n], NN)
            if n == 0:
                proj = (proj + bqv[0:1, place]).astype(bf16).astype(f32) * (HD ** -0.5)
            elif n == 2:
                proj = proj + bqv[1:2, place]
            QKV[rows, n * HC:(n + 1) * HC] = proj.astype(bf16)
        before_heads()
        acc = None
        kept = KEEP[i:i + 1, :]
        real = lax.broadcasted_iota(jnp.int32, (1, IR), 1) % LR < SR
        bias = jnp.where(kept > 0.0, 0.0, jnp.where(real, MASKED, PADDED))
        for h in range(HC // HD):
            pick = lane_head == h
            keys = jnp.where(pick, QKV[rows, HC:2 * HC], zero)
            scores = dot(QKV[rows, 0:HC], keys, NT)
            scores = scores * kept + bias
            expo = jnp.exp(scores - jnp.max(scores, axis=-1, keepdims=True))
            probs = (expo * (1.0 / jnp.sum(expo, axis=-1, keepdims=True))).astype(bf16)
            PR[i * (HC // HD) + h] = probs
            values = jnp.where(pick, QKV[rows, 2 * HC:3 * HC], zero)
            part = dot(probs, values, NN)
            acc = part if acc is None else acc + part
        ATT[rows, :] = acc.astype(bf16)
        before_out()
        rs_ready(0, i)
        for far in (True, False):
            prow = pair(i, (1 - x) if far else x)
            def body(cols):
                PART[prow, cols] = dot(ATT[prow, :], columns(Wo, cols.start, cols.size), NN).astype(bf16)
            over_columns(D, TC, body)
            rs_send(0, i, far)

    def f_norm2(i):
        middle = TOK[local(i), :].astype(f32) + rs_finish(0, i) + bout[...]
        MID[local(i), :] = middle
        N2[block(i, own_t), :] = layer_norm(middle, ln2g[...], ln2s[...])[0].astype(bf16)
        ag_start(1, N2, i)

    def f_feed(i):
        rows = pl.ds(i * IR, IR)
        ag_wait(1, i)
        def body(cols):
            pre = dot(N2[rows, :], W1[:, cols], NN) + bfc1[0:1, aligned(tensor * UC + cols.start, cols.size)]
            sigma = jax.nn.sigmoid(GELU * pre)
            act = pre * sigma
            ACT[rows, cols] = act.astype(bf16)
            DAC[rows, cols] = (sigma + GELU * act * (1.0 - sigma)).astype(bf16)
        over_columns(UC, 256, body)

    def f_feed_out(i, late):
        if not late:
            rs_ready(1, i)
        cols = late_cols if late else early_cols
        first_block = ((1 - half) if late else half) * (D // 256)
        blocks = jnp.concatenate([W2[first_block + n] for n in range(D // 256)], axis=1)
        for far in (True, False):
            prow = pair(i, (1 - x) if far else x)
            PART[prow, cols] = dot(ACT[prow, :], blocks, NN).astype(bf16)
            rs_send(1, i, far, cols)

    sums = {}

    def add(name, value):
        sums[name] = value if name not in sums else sums[name] + value

    def f_final(i, factor):
        final = MID[local(i), :] + rs_finish(1, i) + bfc2[...]
        out[:, i, :] = final[:SR].astype(bf16)
        difference = final - N3[block(i, own_t), :].astype(f32)
        masked = difference * RM[local(i), 0:1]
        add("loss", jnp.sum(jnp.sum(masked * difference, axis=0, keepdims=True), axis=1, keepdims=True))
        grad_final = masked * factor
        DIF[local(i), :] = grad_final
        add("b_fc2", rowsum(grad_final))
        N3[block(i, own_t), :] = grad_final.astype(bf16)
        ag_start(2, N3, i)

    def b_feed(i):
        rows = pl.ds(i * IR, IR)
        def body(cols):
            grad = dot(N3[rows, :], columns(W2, 0, D, cols), NT) * DAC[rows, cols].astype(f32)
            grad = grad.astype(bf16)
            DAC[rows, cols] = grad
            total = rowsum(grad.astype(f32))
            USUM[0:1, cols] = total if i == 0 else USUM[0:1, cols] + total
        over_columns(UC, 256, body)
        rs_ready(2, i)
        for far in (True, False):
            prow = pair(i, (1 - x) if far else x)
            def body2(cols):
                PART[prow, cols] = dot(DAC[prow, :], W1[cols, :], NT).astype(bf16)
            over_columns(D, TC, body2)
            rs_send(2, i, far)

    def b_norm2(i):
        middle = MID[local(i), :]
        _, scaled, inverse = layer_norm(middle, ln2g[...], ln2s[...])
        upstream = rs_finish(2, i)
        add("ln2g", rowsum(upstream * scaled))
        add("ln2s", rowsum(upstream))
        grad_middle = DIF[local(i), :] + norm_backward(upstream, scaled, inverse, ln2g[...])
        DIF[local(i), :] = grad_middle
        add("b_out", rowsum(grad_middle))
        N4[block(i, own_t), :] = grad_middle.astype(bf16)
        ag_start(3, N4, i)

    def b_attention(i, before_head):
        rows = pl.ds(i * IR, IR)
        GA[...] = dot(N4[rows, :], columns(Wo, 0, D), NT).astype(bf16)
        grad = GA[...]
        weighed = grad.astype(f32) * ATT[rows, :].astype(f32)
        query_t = QKV[rows, 0:HC].T
        grad_t = grad.T
        acc, keys_t, values_t = None, [], []
        for h in range(HC // HD):
            pick = lane_head == h
            before_head(h)
            row_dot = jnp.sum(jnp.where(pick, weighed, 0.0), axis=-1, keepdims=True)
            values = jnp.where(pick, QKV[rows, 2 * HC:3 * HC], zero)
            grad_probs = dot(grad, values, NT)
            probs = PR[i * (HC // HD) + h]
            grad_scores = (probs.astype(f32) * ((grad_probs - row_dot) * KEEP[i:i + 1, :])).astype(bf16)
            keys = jnp.where(pick, QKV[rows, HC:2 * HC], zero)
            part = dot(grad_scores, keys, NN)
            acc = part if acc is None else acc + part
            keys_t.append(dot(query_t[h * HD:(h + 1) * HD, :], grad_scores, NN))
            values_t.append(dot(grad_t[h * HD:(h + 1) * HD, :], probs, NN))
        grad_query = (acc * (HD ** -0.5)).astype(bf16)
        grad_key = jnp.concatenate(keys_t, axis=0).astype(bf16).T
        grad_value = jnp.concatenate(values_t, axis=0).astype(bf16).T
        GP[rows, 0:HC] = grad_query
        GP[rows, HC:2 * HC] = grad_key
        GP[rows, 2 * HC:3 * HC] = grad_value
        add("b_q", rowsum(grad_query.astype(f32)))
        add("b_v", rowsum(grad_value.astype(f32)))
        rs_ready(3, i)
        for far in (True, False):
            prow = pair(i, (1 - x) if far else x)
            def body2(cols):
                PART[prow, cols] = dot(GP[prow, :], jnp.concatenate([Wq[n, cols, :] for n in range(3)], axis=1), NT).astype(bf16)
            over_columns(D, TC, body2)
            rs_send(3, i, far)

    def b_norm1(i):
        _, scaled, inverse = layer_norm(TOK[local(i), :].astype(f32), ln1g[...], ln1s[...])
        upstream = rs_finish(3, i)
        add("ln1g", rowsum(upstream * scaled))
        add("ln1s", rowsum(upstream))
        grad = DIF[local(i), :] + norm_backward(upstream, scaled, inverse, ln1g[...])
        gtok[:, i, :] = grad[:SR]

    def nothing():
        pass

    images = list(range(I))
    first, last = images[0], images[-1]
    counting = count_start()
    weight_send(0)
    weight_own(0)
    weight_send(1)
    weight_send(2)
    weight_send(3)
    for i in images:
        f_norm1(i)
    prepare_masks()
    for i in images:
        prepare_teacher(i)
    weight_forward(0, 1)
    ag_forward(0, N1, first)
    weight_forward(0, 2)
    for i in images[1:]:
        ag_forward(0, N1, i)
    weight_forward(0, 3)
    weight_own(1)
    weight_wait(0)

    def out_forward():
        weight_forward(1, 1, 2, 3)
        weight_own(2)
        weight_own(3)

    for i in images:
        ag_wait(0, i)
        if i == first:
            f_attention(i, out_forward, lambda: weight_wait(1))
        else:
            f_attention(i, nothing, nothing)
        rs_mid(0, i)
        if i == first:
            weight_forward(2, 1)
    weight_forward(2, 2)
    f_norm2(first)
    weight_forward(2, 3)
    for i in images[1:]:
        f_norm2(i)
    counting = count_next(counting)
    ag_forward(1, N2, first)
    weight_forward(3, 1)
    weight_wait(2)
    f_feed(first)
    for i in images[1:]:
        ag_forward(1, N2, i)
        weight_forward(3, 2)
        f_feed(i)
    weight_wait(3, 0, 1)
    for i in images:
        f_feed_out(i, False)
    weight_forward(3, 3)
    for i in images:
        rs_mid(1, i, early_cols)
    weight_wait(3, 2, 3)
    for i in images:
        f_feed_out(i, True)
    for i in images:
        rs_mid(1, i, late_cols)
    count = count_end(counting)
    normalizer = count * float(D)
    factor = lscale[...] * 2.0 / normalizer
    for i in images:
        f_final(i, factor)
    for i in images:
        ag_forward(2, N3, i)
        ag_wait(2, i)
        if i == last:
            weight_grad(3, ACT, N3)
        b_feed(i)
        rs_mid(2, i)
    weight_grad(2, N2, DAC)
    grad_a(3, 3)
    b_norm2(first)
    grad_a(3, 1)
    for i in images[1:]:
        b_norm2(i)
    grad_b(3)

    for n in range(4):
        VTE[tensor, n:n + 1, :] = jnp.where(tensor == n, USUM[0:1, :], 0.0)
    for n, name in enumerate(("ln2g", "ln2s", "b_fc2", "b_out")):
        VTE[tensor, 4 + n:5 + n, :] = sums[name]
    VTE[tensor, 8:9, :] = jnp.broadcast_to(sums["loss"], (1, D))
    VTE[tensor, 9:16, :] = jnp.zeros((7, D), f32)
    early = vector_sum(VTE, VSE, VPE, VDE, True)
    advance(early)

    def progress(i, h):
        if i == first and h == 3:
            grad_a(2, 3)
        if i == last and h == 2:
            grad_b(2)

    for i in images:
        ag_forward(3, N4, i)
        ag_wait(3, i)
        if i == last:
            grad_a(2, 1)
            advance(early)
            weight_grad(1, ATT, N4)
        b_attention(i, functools.partial(progress, i))
        rs_mid(3, i)
    weight_grad(0, N1, GP)
    b_norm1(first)
    grad_a(1, 3, 1)
    grad_b(1)
    grad_a(0, 3)
    for i in images[1:]:
        b_norm1(i)
    VTL[tensor] = jnp.zeros((8, D), f32)
    VTL[tensor, 0:1, :] = sums["ln1g"]
    VTL[tensor, 1:2, :] = sums["ln1s"]
    VTL[tensor, 2:3, aligned(tensor * HC, HC)] = sums["b_q"]
    VTL[tensor, 3:4, aligned(tensor * HC, HC)] = sums["b_v"]
    late = vector_sum(VTL, VSL, VPL, VDL, False)
    advance(late)
    grad_a(0, 1)
    advance(late)
    grad_b(0)
    advance(early)
    grad_end(3)
    grad_end(2)
    grad_end(1)

    def cut(V, row, count):
        part = V[8, row:row + count, :]
        picked = jnp.zeros((count, 32), f32)
        for t in range(4):
            picked = jnp.where(tensor == t, part[:, 32 * t:32 * t + 32], picked)
        return picked

    if inside:
        small[...] = jnp.zeros(small.shape, f32)
        small[0:1, :] = VDE[8, 0:1, :]
        small[1:5, 0:32] = cut(VDE, 4, 4)
        small[5:6, :] = VDE[8, 8:9, :] / normalizer
        advance(late)
        small[6:10, 0:32] = cut(VDL, 0, 4)
    else:
        small[0:16, :] = VSE[...]
        small[8:9, :] = VSE[8:9, :] / normalizer
        small[16:24, :] = VSL[...]
    grad_end(0)
    net.finish()


def body(
    mesh_dp, tokens, valid_mask, teacher, loss_scale, ln1_gain, ln1_shift, w_qkv, b_qv, w_out, b_out,
    ln2_gain, ln2_shift, w_fc1, b_fc1, w_fc2, b_fc2,
):
    rows, I, D = tokens.shape
    seq = valid_mask.shape[0]
    parts = seq // rows
    HC, UC = w_qkv.shape[2], w_fc1.shape[1]
    LR = -(-rows // 16) * 16
    IR = parts * LR
    inside = mesh_dp == 8
    part = lax.axis_index("tensor")

    NB = D // 128
    if inside:
        count = loss_scale
        weights = (jnp.transpose(w_qkv, (1, 0, 2)), w_out, w_fc1, w_fc2)
        gdt = f32
    else:
        count = lax.psum(jnp.sum(valid_mask.astype(f32)), "dp")

        def blocks(values):
            full = lax.all_gather(values, "dp", axis=1, tiled=True)
            return jnp.transpose(full.reshape(-1, NB, 128), (1, 0, 2))

        weights = (
            jnp.transpose(lax.all_gather(w_qkv, "dp", axis=0, tiled=True), (1, 0, 2)),
            blocks(w_out),
            lax.all_gather(w_fc1, "dp", axis=0, tiled=True),
            blocks(w_fc2),
        )
        gdt = bf16
    KS = w_fc1.shape[0]
    flat = [v.reshape(1, -1) for v in (ln1_gain, ln1_shift, ln2_gain, ln2_shift, b_out, b_fc2, b_fc1)]
    size = dict(I=I, LR=LR, SR=rows, IR=IR, D=D, HC=HC, UC=UC, KS=KS, inside=inside)
    H = HC // HD
    VM = pltpu.VMEM
    if inside:
        gshapes = [(3, KS, HC), (HC, KS), (KS, UC), (UC, KS)]
    else:
        gshapes = [(3, D, HC), (NB, HC, 128), (D, UC), (NB, UC, 128)]
    k4, k3 = (4, 3) if inside else (1, 1)
    part_shapes = gshapes if inside else [(16, 128)] * 4
    scratch = [
        VM((3, D, HC), bf16), VM((NB, HC, 128), bf16), VM((D, UC), bf16), VM((NB, UC, 128), bf16),
        VM((I * IR, D), bf16), VM((I * IR, D), bf16), VM((I * IR, D), bf16), VM((I * IR, D), bf16),
        VM((I * IR, 3 * HC), bf16), VM((I * H, IR, IR), bf16), VM((I * IR, HC), bf16),
        VM((I * IR, UC), bf16), VM((I * IR, UC), bf16), VM((IR, HC), bf16), VM((I * IR, 3 * HC), bf16),
        VM((I * IR, D), bf16), VM((2 * I * LR, D), bf16), VM((I * LR, D), bf16), VM((I * LR, D), bf16),
        VM((I * LR, D), f32), VM((I * LR, D), f32),
        VM((3, D, HC), bf16), VM((NB, HC, 128), bf16), VM((D, UC), bf16), VM((NB, UC, 128), bf16),
    ]
    scratch += [VM((k4,) + s, bf16) for s in part_shapes]
    scratch += [VM((k3,) + s, bf16) for s in part_shapes]
    scratch += [
        VM((I * LR, D), bf16), VM((8, IR), f32), VM((I * LR, 128), f32), VM((8, UC), f32),
        VM((4, 16, D), f32), VM((16, D), f32), VM((8, 16, 128), f32), VM((9, 16, 128), f32),
        VM((4, 8, D), f32), VM((8, D), f32), VM((8, 8, 128), f32), VM((9, 8, 128), f32),
        VM((6, 8, 128), f32),
        pltpu.SemaphoreType.DMA((4,)), pltpu.SemaphoreType.DMA((150,)), pltpu.SemaphoreType.DMA((150,)),
    ]
    vm, hbm = pl.BlockSpec(memory_space=pltpu.VMEM), pl.BlockSpec(memory_space=pl.ANY)
    shape = jax.ShapeDtypeStruct
    results = pl.pallas_call(
        functools.partial(kernel, size),
        out_shape=[shape((rows, I, D), bf16), shape((rows, I, D), f32)]
        + [shape(s, gdt) for s in gshapes]
        + [shape((16, 128) if inside else (24, D), f32)],
        in_specs=[vm] * 13 + [hbm] * 4,
        out_specs=[vm] * 7,
        scratch_shapes=scratch,
        compiler_params=pltpu.CompilerParams(
            collective_id=0, has_side_effects=True, vmem_limit_bytes=64 * 2 ** 20 - 2 ** 16
        ),
    )(tokens, teacher, valid_mask.T, *flat, b_qv, loss_scale.reshape(1, 1), count.reshape(1, 1), *weights)
    out, gtok, gq, go, g1, g2, small = results

    n = D // (mesh_dp * parts)
    gq = jnp.transpose(gq, (1, 0, 2))
    if inside:
        units_cut = small[0]
        cut = small[:, :n]
    else:
        def whole(values):
            full = jnp.transpose(values, (1, 0, 2)).reshape(-1, D)
            return lax.psum_scatter(full, "dp", scatter_dimension=1, tiled=True).astype(f32)

        index = lax.axis_index("dp") * parts + part
        gq = lax.psum_scatter(gq, "dp", scatter_dimension=0, tiled=True).astype(f32)
        g1 = lax.psum_scatter(g1, "dp", scatter_dimension=0, tiled=True).astype(f32)
        go, g2 = whole(go), whole(g2)
        small = lax.psum(small, "dp")
        cut = lax.dynamic_slice_in_dim(small, index * n, n, 1)
        cut = jnp.concatenate([cut[3:9], cut[16:20]], axis=0)
        m = UC // mesh_dp
        units_cut = lax.dynamic_slice_in_dim(small[0:parts].reshape(-1), index * m, m, 0)
    return (
        out, small[5, 0] if inside else small[8, 0], gtok, cut[6], cut[7], gq, cut[8:10], go,
        cut[4], cut[1], cut[2], g1, units_cut, g2, cut[3],
    )


def solution(mesh):
    in_specs = (
        P("tensor", "dp", None), P(None, "dp"), P("tensor", "dp", None), P(), P(), P(),
        P("dp", None, "tensor"), P(), P("tensor", "dp"), P(), P(), P(), P("dp", "tensor"), P(),
        P("tensor", "dp"), P(),
    )
    both = ("dp", "tensor")
    out_specs = (
        P("tensor", "dp", None), P(), P("tensor", "dp", None), P(both), P(both), P("dp", None, "tensor"),
        P(None, both), P("tensor", "dp"), P(both), P(both), P(both), P("dp", "tensor"), P(both),
        P("tensor", "dp"), P(both),
    )
    return jax.shard_map(
        functools.partial(body, mesh.shape["dp"]), mesh=mesh, in_specs=in_specs, out_specs=out_specs,
        check_vma=False,
    )
```

```python
import functools

import jax
import jax.numpy as jnp
from jax import lax
from jax.experimental import pallas as pl
from jax.experimental.pallas import tpu as pltpu
from jax.sharding import PartitionSpec as P

HD = 64
EPS = 1e-05
MASKED = -1000000000.0
PADDED = -3000000000.0
GELU = 1.702
MESH = pl.DeviceIdType.MESH
f32 = jnp.float32
bf16 = jnp.bfloat16
NN = (((1,), (0,)), ((), ()))
NT = (((1,), (1,)), ((), ()))
TN = (((0,), (0,)), ((), ()))

def dot(a, b, dims):
    return lax.dot_general(a, b, dims, preferred_element_type=f32)


def layer_norm(values, gain, shift):
    center = values - jnp.mean(values, axis=-1, keepdims=True)
    inverse = lax.rsqrt(jnp.mean(center * center, axis=-1, keepdims=True) + EPS)
    scaled = center * inverse
    return scaled * gain + shift, scaled, inverse


def norm_backward(upstream, scaled, inverse, gain):
    weighted = upstream * gain
    inner = weighted - jnp.mean(weighted, axis=-1, keepdims=True)
    inner = inner - scaled * jnp.mean(weighted * scaled, axis=-1, keepdims=True)
    return inverse * inner


def rowsum(values):
    return jnp.sum(values, axis=0, keepdims=True)


def aligned(start, size):
    if isinstance(start, int):
        return pl.ds(start, size)
    return pl.ds(pl.multiple_of(start, size), size)


class Copies:
    def __init__(self, send, recv):
        self.send, self.recv, self.count = send, recv, 0
        self.all = []

    def make(self, src, dst, device):
        copy = pltpu.make_async_remote_copy(
            src_ref=src,
            dst_ref=dst,
            send_sem=self.send.at[self.count],
            recv_sem=self.recv.at[self.count],
            device_id=device,
            device_id_type=MESH,
        )
        self.count += 1
        return copy

    def start(self, src, dst, device):
        copy = self.make(src, dst, device)
        copy.start()
        self.all.append(copy)
        return copy

    def wait_send(self, copy):
        copy.wait_send()
        self.all = [other for other in self.all if other is not copy]

    def finish(self):
        for copy in self.all:
            copy.wait_send()
        self.all = []


def kernel(
    size,
    tok, tea, mask, ln1g, ln1s, ln2g, ln2s, bout, bfc2, bfc1, bqv, lscale, given, wq, wo, w1, w2,
    out, gtok, gq, go, g1, g2, small,
    Wq, Wo, W1, W2, N1, N2, N3, N4, QKV, PR, ATT, ACT, DAC, GA, GP, PART, RA, RX, XS, MID, DIF,
    GWq, GWo, GW1, GW2, YRq, YRo, YR1, YR2, ZRq, ZRo, ZR1, ZR2,
    TOK, KEEP, RM, USUM, VTE, VSE, VPE, VDE, VTL, VSL, VPL, VDL, CN, local_sem, send_sem, recv_sem,
):
    I, LR, IR, D, HC, UC = size["I"], size["LR"], size["IR"], size["D"], size["HC"], size["UC"]
    inside = size["inside"]
    KS, SR = size["KS"], size["SR"]
    dp, tensor = lax.axis_index("dp"), lax.axis_index("tensor")
    z, y, x, c = dp // 2, dp % 2, tensor // 2, tensor % 2
    mate = (dp, x * 2 + 1 - c)
    xnei = (dp, (1 - x) * 2 + c)
    diag = (dp, (1 - x) * 2 + 1 - c)
    ynei = (z * 2 + 1 - y, tensor)

    def zat(k):
        return (z, z + 1 - 2 * (z % 2), lax.rem(z + 2, 4), 3 - z)[k]

    def zdev(k):
        return (zat(k) * 2 + y, tensor)

    net = Copies(send_sem, recv_sem)

    barrier = pltpu.get_barrier_semaphore()
    group = [zat(k) * 2 + y for k in (1, 2, 3)] + [zat(k) * 2 + 1 - y for k in (0, 1, 2, 3)]
    peers = [mate, xnei, diag] + ([(other, tensor) for other in group] if inside else [])
    for peer in peers:
        pl.semaphore_signal(barrier, inc=1, device_id=peer, device_id_type=MESH)
    pl.semaphore_wait(barrier, len(peers))

    weights = [(wq, Wq, 0, YRq, ZRq, GWq, gq), (wo, Wo, 1, YRo, ZRo, GWo, go),
               (w1, W1, 2, YR1, ZR1, GW1, g1), (w2, W2, 1, YR2, ZR2, GW2, g2)]

    def shard(ref, kind, index):
        if kind == 1:
            return ref.at[index]
        place = pl.ds(pl.multiple_of(index * KS, KS), KS)
        return ref.at[:, place, :] if kind == 0 else ref.at[place, :]

    def columns(ref, start, count, rows=slice(None)):
        return jnp.concatenate([ref[n, rows, :] for n in range(start // 128, (start + count) // 128)], axis=1)

    gathers = {}
    locals_ = []

    def weight_send(w):
        arg, full, axis = weights[w][:3]
        mine = shard(full, axis, dp) if inside else full
        copy = pltpu.make_async_copy(arg, mine, local_sem.at[w])
        copy.start()
        locals_.append(copy)
        if inside:
            gathers[w] = {k: net.start(arg, mine, zdev(k)) for k in (1, 2, 3)}, {}

    def weight_own(w):
        if inside:
            arg, full, axis = weights[w][:3]
            gathers[w][1][0] = net.start(arg, shard(full, axis, dp), ynei)

    def weight_forward(w, *ks):
        if not inside:
            return
        full, axis = weights[w][1:3]
        zs, ys = gathers[w]
        for k in ks:
            zs[k].wait_recv()
            got = shard(full, axis, zat(k) * 2 + y)
            ys[k] = net.start(got, got, ynei)

    def weight_wait(w, *ks):
        ks = ks or (0, 1, 2, 3)
        if 0 in ks:
            locals_[w].wait()
        if inside:
            for k in ks:
                gathers[w][1][k].wait_recv()

    scatters = {w: ({}, {}) for w in range(4)}
    order = (3, 1, 2, 0)

    def grad_y(w, k):
        if inside:
            axis, YR, GW = weights[w][2], weights[w][3], weights[w][5]
            scatters[w][0][k] = net.start(shard(GW, axis, zat(k) * 2 + 1 - y), YR.at[k], ynei)

    def weight_grad(w, lhs, rhs, hold=()):
        GW = weights[w][5]
        step = D // 4
        for k in order:
            group = zat(k) if inside else k
            place = aligned(group * step, step)
            if w == 0:
                part = dot(lhs[:, place], rhs[...], TN).astype(bf16)
                for n in range(3):
                    GW[n, place, :] = part[:, n * HC:(n + 1) * HC]
            elif w == 2:
                GW[place, :] = dot(lhs[:, place], rhs[...], TN).astype(bf16)
            else:
                part = dot(lhs[...], rhs[:, place], TN).astype(bf16)
                GW[group * 2] = part[:, :128]
                GW[group * 2 + 1] = part[:, 128:]
            if k not in hold:
                grad_y(w, k)

    def zfirst_send(w):
        if inside:
            axis, YR, GW = weights[w][2], weights[w][3], weights[w][5]
            for yy, slot in ((1 - y, 0), (y, 1)):
                for k in (3, 1):
                    part = shard(GW, axis, zat(k) * 2 + yy)
                    place = YR.at[(0 if k == 3 else 2) + slot]
                    scatters[w][0][k, slot] = net.start(part, place, zdev(1))

    def zfirst_a(w, k):
        if not inside:
            return
        axis, YR, ZR, GW = weights[w][2:6]
        scatters[w][0][1 + k, 0].wait_recv()
        place = shard(GW, axis, zat(k) * 2 + 1 - y)
        place[...] = (place[...].astype(f32) + YR[2 - k].astype(f32)).astype(bf16)
        scatters[w][1][k] = net.start(place, ZR.at[1 - k // 2], ynei)

    def zfirst_b(w):
        if not inside:
            return
        axis, YR, ZR, GW = weights[w][2:6]
        scatters[w][0][3, 1].wait_recv()
        scatters[w][1][2].wait_recv()
        place = shard(GW, axis, zat(2) * 2 + y)
        total = place[...].astype(f32) + YR[1].astype(f32) + ZR[0].astype(f32)
        place[...] = total.astype(bf16)
        scatters[w][1][3] = net.start(place, ZR.at[2], zdev(2))

    def zfirst_end(w):
        axis, YR, ZR, GW, result = weights[w][2:7]
        if not inside:
            result[...] = GW[...]
            return
        scatters[w][0][1, 1].wait_recv()
        scatters[w][1][0].wait_recv()
        scatters[w][1][3].wait_recv()
        total = shard(GW, axis, dp)[...].astype(f32) + YR[3].astype(f32)
        result[...] = total + ZR[1].astype(f32) + ZR[2].astype(f32)

    def grad_a(w, *ks):
        if not inside:
            return
        axis, YR, ZR, GW = weights[w][2:6]
        for k in ks:
            scatters[w][0][k].wait_recv()
            place = shard(GW, axis, zat(k) * 2 + y)
            place[...] = (place[...].astype(f32) + YR[k].astype(f32)).astype(bf16)
            scatters[w][1][k] = net.start(place, ZR.at[k // 2], zdev(1))

    def grad_b(w):
        if not inside:
            return
        axis, YR, ZR, GW = weights[w][2:6]
        scatters[w][0][2].wait_recv()
        scatters[w][1][3].wait_recv()
        place = shard(GW, axis, zat(2) * 2 + y)
        total = place[...].astype(f32) + YR[2].astype(f32) + ZR[1].astype(f32)
        place[...] = total.astype(bf16)
        scatters[w][1][2] = net.start(place, ZR.at[2], zdev(2))

    def grad_end(w):
        axis, YR, ZR, GW, result = weights[w][2:7]
        if not inside:
            result[...] = GW[...]
            return
        scatters[w][0][0].wait_recv()
        scatters[w][1][1].wait_recv()
        scatters[w][1][2].wait_recv()
        total = shard(GW, axis, dp)[...].astype(f32) + YR[0].astype(f32)
        result[...] = total + ZR[0].astype(f32) + ZR[2].astype(f32)

    def vector_sum(VT, VS, VP, VD, units):
        copies = [net.start(VT.at[tensor], VT.at[tensor], peer) for peer in (mate, xnei, diag)]
        yield
        for copy in copies:
            copy.wait_recv()
        VS[...] = (VT[0] + VT[1]) + (VT[2] + VT[3])
        if not inside:
            return
        for d in range(8):
            VP[d] = VS[:, d * 128:(d + 1) * 128]
            if units:
                VP[d, 0:1, :] = VS[d // 2:d // 2 + 1, aligned((d % 2 * 4 + tensor) * 128, 128)]
        VD[dp] = VP[dp]
        copies = [net.start(VP.at[other], VD.at[dp], (other, tensor)) for other in group]
        yield
        for copy in copies:
            copy.wait_recv()
        VD[8] = ((VD[0] + VD[1]) + (VD[2] + VD[3])) + ((VD[4] + VD[5]) + (VD[6] + VD[7]))

    def advance(steps):
        next(steps, None)

    def count_start():
        if not inside:
            return None
        CN[z] = jnp.broadcast_to(jnp.sum(mask[...].astype(f32), keepdims=True), (8, 128))
        return [net.start(CN.at[z], CN.at[z], zdev(k)) for k in (1, 2, 3)]

    def count_next(copies):
        if not inside:
            return None
        for copy in copies:
            copy.wait_recv()
        CN[4] = (CN[0] + CN[1]) + (CN[2] + CN[3])
        return net.start(CN.at[4], CN.at[5], ynei)

    def count_end(copy):
        if not inside:
            return given[...]
        copy.wait_recv()
        return CN[4, 0:1, 0:1] + CN[5, 0:1, 0:1]

    def block(i, t):
        return aligned((i * 4 + t) * LR, LR)

    def local(i):
        return pl.ds(i * LR, LR)

    def pair(i, xx):
        return aligned(i * IR + xx * 2 * LR, 2 * LR)

    own_t, other_t = tensor, (1 - x) * 2 + c
    ag, rs = {}, {}

    def ag_start(s, N, i):
        mine = N.at[block(i, own_t), :]
        ag[s, i] = [net.start(mine, mine, xnei), net.start(mine, mine, mate)]

    def ag_forward(s, N, i):
        ag[s, i][0].wait_recv()
        got = N.at[block(i, other_t), :]
        ag[s, i].append(net.start(got, got, mate))

    def ag_wait(s, i):
        ag[s, i][1].wait_recv()
        ag[s, i][2].wait_recv()

    def landing(ref, n):
        return ref.at[pl.ds(n * LR, LR), :]

    half = (z // 2) if inside else 0
    early_cols, late_cols = aligned(half * (D // 2), D // 2), aligned((1 - half) * (D // 2), D // 2)
    all_cols = pl.ds(0, D)

    def rs_ready(s, i):
        for copies in rs.get((s - 1, i), []):
            for copy in copies[:2]:
                net.wait_send(copy)

    def rs_send(s, i, far, cols=all_cols):
        base = i * IR + ((1 - x) if far else x) * 2 * LR
        src = PART.at[aligned(base + (1 - c) * LR, LR), cols]
        dst = RA.at[pl.ds((i * 2 + (0 if far else 1)) * LR, LR), cols]
        if far:
            rs.setdefault((s, i), []).append([])
        rs[s, i][-1].append(net.start(src, dst, mate))

    def rs_mid(s, i, cols=all_cols):
        copies = rs[s, i][-1]
        copies[0].wait_recv()
        if len(rs[s, i]) == 1:
            for before in rs.get((s - 1, i), []):
                net.wait_send(before[2])
        kept = PART[aligned(i * IR + (1 - x) * 2 * LR + c * LR, LR), cols]
        got = RA[pl.ds(i * 2 * LR, LR), cols]
        XS[local(i), cols] = (kept.astype(f32) + got.astype(f32)).astype(bf16)
        copies.append(net.start(XS.at[local(i), cols], RX.at[local(i), cols], xnei))

    def rs_finish(s, i):
        for copies in rs[s, i]:
            copies[1].wait_recv()
            copies[2].wait_recv()
        kept = PART[aligned(i * IR + x * 2 * LR + c * LR, LR), :].astype(f32)
        return kept + landing(RA, i * 2 + 1)[...].astype(f32) + RX[local(i), :].astype(f32)

    def prepare_teacher(i):
        start = (i * 4 + own_t) * LR
        N3[aligned(start + SR // 16 * 16, 16), :] = jnp.zeros((16, D), bf16)
        N3[pl.ds(pl.multiple_of(start, LR), SR), :] = tea[:, i, :]

    def prepare_masks():
        KEEP[...] = jnp.zeros(KEEP.shape, f32)
        for t in range(4):
            KEEP[0:I, t * LR:t * LR + SR] = mask[:, t * SR:(t + 1) * SR].astype(f32)
        near = lax.broadcasted_iota(jnp.int32, (LR, LR), 0) == lax.broadcasted_iota(jnp.int32, (LR, LR), 1)
        for i in range(I):
            row = jnp.zeros((1, LR), f32)
            for t in range(4):
                row = jnp.where(tensor == t, KEEP[i:i + 1, t * LR:(t + 1) * LR], row)
            RM[local(i), 0:1] = jnp.sum(jnp.where(near, row, 0.0), axis=1, keepdims=True)

    TC = 512 if D % 512 == 0 and UC % 512 == 0 else 256

    def over_columns(n, step, body):
        for j in range(n // step):
            body(pl.ds(j * step, step))

    def f_norm1(i):
        TOK[i * LR + SR // 16 * 16:(i + 1) * LR, :] = jnp.zeros((LR - SR // 16 * 16, D), bf16)
        TOK[i * LR:i * LR + SR, :] = tok[:, i, :]
        normed = layer_norm(TOK[local(i), :].astype(f32), ln1g[...], ln1s[...])[0]
        N1[block(i, own_t), :] = normed.astype(bf16)
        ag_start(0, N1, i)

    lane_head = lax.broadcasted_iota(jnp.int32, (1, HC), 1) // HD
    zero = jnp.zeros((), bf16)

    def f_attention(i, before_heads, before_out):
        rows = pl.ds(i * IR, IR)
        place = aligned(tensor * HC, HC)
        for n in range(3):
            proj = dot(N1[rows, :], Wq[n], NN)
            if n == 0:
                proj = (proj + bqv[0:1, place]).astype(bf16).astype(f32) * (HD ** -0.5)
            elif n == 2:
                proj = proj + bqv[1:2, place]
            QKV[rows, n * HC:(n + 1) * HC] = proj.astype(bf16)
        before_heads()
        acc = None
        kept = KEEP[i:i + 1, :]
        real = lax.broadcasted_iota(jnp.int32, (1, IR), 1) % LR < SR
        bias = jnp.where(kept > 0.0, 0.0, jnp.where(real, MASKED, PADDED))
        for h in range(HC // HD):
            pick = lane_head == h
            keys = jnp.where(pick, QKV[rows, HC:2 * HC], zero)
            scores = dot(QKV[rows, 0:HC], keys, NT)
            scores = scores * kept + bias
            expo = jnp.exp(scores - jnp.max(scores, axis=-1, keepdims=True))
            probs = (expo * (1.0 / jnp.sum(expo, axis=-1, keepdims=True))).astype(bf16)
            PR[i * (HC // HD) + h] = probs
            values = jnp.where(pick, QKV[rows, 2 * HC:3 * HC], zero)
            part = dot(probs, values, NN)
            acc = part if acc is None else acc + part
        ATT[rows, :] = acc.astype(bf16)
        before_out()
        rs_ready(0, i)
        for far in (True, False):
            prow = pair(i, (1 - x) if far else x)
            def body(cols):
                PART[prow, cols] = dot(ATT[prow, :], columns(Wo, cols.start, cols.size), NN).astype(bf16)
            over_columns(D, TC, body)
            rs_send(0, i, far)

    def f_norm2(i):
        middle = TOK[local(i), :].astype(f32) + rs_finish(0, i) + bout[...]
        MID[local(i), :] = middle
        N2[block(i, own_t), :] = layer_norm(middle, ln2g[...], ln2s[...])[0].astype(bf16)
        ag_start(1, N2, i)

    def f_feed(i):
        rows = pl.ds(i * IR, IR)
        ag_wait(1, i)
        def body(cols):
            pre = dot(N2[rows, :], W1[:, cols], NN) + bfc1[0:1, aligned(tensor * UC + cols.start, cols.size)]
            sigma = jax.nn.sigmoid(GELU * pre)
            act = pre * sigma
            ACT[rows, cols] = act.astype(bf16)
            DAC[rows, cols] = (sigma + GELU * act * (1.0 - sigma)).astype(bf16)
        over_columns(UC, 256, body)

    def f_feed_out(i, late):
        if not late:
            rs_ready(1, i)
        cols = late_cols if late else early_cols
        first_block = ((1 - half) if late else half) * (D // 256)
        blocks = jnp.concatenate([W2[first_block + n] for n in range(D // 256)], axis=1)
        for far in (True, False):
            prow = pair(i, (1 - x) if far else x)
            PART[prow, cols] = dot(ACT[prow, :], blocks, NN).astype(bf16)
            rs_send(1, i, far, cols)

    sums = {}

    def add(name, value):
        sums[name] = value if name not in sums else sums[name] + value

    def f_final(i, factor):
        final = MID[local(i), :] + rs_finish(1, i) + bfc2[...]
        out[:, i, :] = final[:SR].astype(bf16)
        difference = final - N3[block(i, own_t), :].astype(f32)
        masked = difference * RM[local(i), 0:1]
        add("loss", jnp.sum(jnp.sum(masked * difference, axis=0, keepdims=True), axis=1, keepdims=True))
        grad_final = masked * factor
        DIF[local(i), :] = grad_final
        add("b_fc2", rowsum(grad_final))
        N3[block(i, own_t), :] = grad_final.astype(bf16)
        ag_start(2, N3, i)

    def b_feed(i):
        rows = pl.ds(i * IR, IR)
        def body(cols):
            grad = dot(N3[rows, :], columns(W2, 0, D, cols), NT) * DAC[rows, cols].astype(f32)
            grad = grad.astype(bf16)
            DAC[rows, cols] = grad
            total = rowsum(grad.astype(f32))
            USUM[0:1, cols] = total if i == 0 else USUM[0:1, cols] + total
        over_columns(UC, 256, body)
        rs_ready(2, i)
        for far in (True, False):
            prow = pair(i, (1 - x) if far else x)
            def body2(cols):
                PART[prow, cols] = dot(DAC[prow, :], W1[cols, :], NT).astype(bf16)
            over_columns(D, TC, body2)
            rs_send(2, i, far)

    def b_norm2(i):
        middle = MID[local(i), :]
        _, scaled, inverse = layer_norm(middle, ln2g[...], ln2s[...])
        upstream = rs_finish(2, i)
        add("ln2g", rowsum(upstream * scaled))
        add("ln2s", rowsum(upstream))
        grad_middle = DIF[local(i), :] + norm_backward(upstream, scaled, inverse, ln2g[...])
        DIF[local(i), :] = grad_middle
        add("b_out", rowsum(grad_middle))
        N4[block(i, own_t), :] = grad_middle.astype(bf16)
        ag_start(3, N4, i)

    def b_attention(i, before_head):
        rows = pl.ds(i * IR, IR)
        GA[...] = dot(N4[rows, :], columns(Wo, 0, D), NT).astype(bf16)
        grad = GA[...]
        weighed = grad.astype(f32) * ATT[rows, :].astype(f32)
        query_t = QKV[rows, 0:HC].T
        grad_t = grad.T
        acc, keys_t, values_t = None, [], []
        for h in range(HC // HD):
            pick = lane_head == h
            before_head(h)
            row_dot = jnp.sum(jnp.where(pick, weighed, 0.0), axis=-1, keepdims=True)
            values = jnp.where(pick, QKV[rows, 2 * HC:3 * HC], zero)
            grad_probs = dot(grad, values, NT)
            probs = PR[i * (HC // HD) + h]
            grad_scores = (probs.astype(f32) * ((grad_probs - row_dot) * KEEP[i:i + 1, :])).astype(bf16)
            keys = jnp.where(pick, QKV[rows, HC:2 * HC], zero)
            part = dot(grad_scores, keys, NN)
            acc = part if acc is None else acc + part
            keys_t.append(dot(query_t[h * HD:(h + 1) * HD, :], grad_scores, NN))
            values_t.append(dot(grad_t[h * HD:(h + 1) * HD, :], probs, NN))
        grad_query = (acc * (HD ** -0.5)).astype(bf16)
        grad_key = jnp.concatenate(keys_t, axis=0).astype(bf16).T
        grad_value = jnp.concatenate(values_t, axis=0).astype(bf16).T
        GP[rows, 0:HC] = grad_query
        GP[rows, HC:2 * HC] = grad_key
        GP[rows, 2 * HC:3 * HC] = grad_value
        add("b_q", rowsum(grad_query.astype(f32)))
        add("b_v", rowsum(grad_value.astype(f32)))
        rs_ready(3, i)
        for far in (True, False):
            prow = pair(i, (1 - x) if far else x)
            def body2(cols):
                PART[prow, cols] = dot(GP[prow, :], jnp.concatenate([Wq[n, cols, :] for n in range(3)], axis=1), NT).astype(bf16)
            over_columns(D, TC, body2)
            rs_send(3, i, far)

    def b_norm1(i):
        _, scaled, inverse = layer_norm(TOK[local(i), :].astype(f32), ln1g[...], ln1s[...])
        upstream = rs_finish(3, i)
        add("ln1g", rowsum(upstream * scaled))
        add("ln1s", rowsum(upstream))
        grad = DIF[local(i), :] + norm_backward(upstream, scaled, inverse, ln1g[...])
        gtok[:, i, :] = grad[:SR]

    def nothing():
        pass

    images = list(range(I))
    first, last = images[0], images[-1]
    counting = count_start()
    weight_send(0)
    weight_own(0)
    weight_send(1)
    weight_send(2)
    weight_send(3)
    for i in images:
        f_norm1(i)
    prepare_masks()
    for i in images:
        prepare_teacher(i)
    weight_forward(0, 1)
    ag_forward(0, N1, first)
    weight_forward(0, 2)
    for i in images[1:]:
        ag_forward(0, N1, i)
    weight_forward(0, 3)
    weight_own(1)
    weight_wait(0)

    def out_forward():
        weight_forward(1, 1, 2, 3)
        weight_own(2)
        weight_own(3)

    for i in images:
        ag_wait(0, i)
        if i == first:
            f_attention(i, out_forward, lambda: weight_wait(1))
        else:
            f_attention(i, nothing, nothing)
        rs_mid(0, i)
        if i == first:
            weight_forward(2, 1)
    weight_forward(2, 2)
    f_norm2(first)
    weight_forward(2, 3)
    for i in images[1:]:
        f_norm2(i)
    counting = count_next(counting)
    ag_forward(1, N2, first)
    weight_forward(3, 1)
    weight_wait(2)
    f_feed(first)
    for i in images[1:]:
        ag_forward(1, N2, i)
        weight_forward(3, 2)
        f_feed(i)
    weight_wait(3, 0, 1)
    for i in images:
        f_feed_out(i, False)
        if i == first:
            weight_forward(3, 3)
    for i in images:
        rs_mid(1, i, early_cols)
    weight_wait(3, 2, 3)
    for i in images:
        f_feed_out(i, True)
    for i in images:
        rs_mid(1, i, late_cols)
    count = count_end(counting)
    normalizer = count * float(D)
    factor = lscale[...] * 2.0 / normalizer
    for i in images:
        f_final(i, factor)
    for i in images:
        ag_forward(2, N3, i)
        ag_wait(2, i)
        if i == last:
            weight_grad(3, ACT, N3, (0, 1, 2, 3))
            zfirst_send(3)
        b_feed(i)
        rs_mid(2, i)
    weight_grad(2, N2, DAC, (2, 0))
    zfirst_a(3, 2)
    b_norm2(first)
    zfirst_a(3, 0)
    grad_y(2, 2)
    grad_y(2, 0)
    for i in images[1:]:
        b_norm2(i)
    grad_a(2, 3, 1)

    for n in range(4):
        VTE[tensor, n:n + 1, :] = jnp.where(tensor == n, USUM[0:1, :], 0.0)
    for n, name in enumerate(("ln2g", "ln2s", "b_fc2", "b_out")):
        VTE[tensor, 4 + n:5 + n, :] = sums[name]
    VTE[tensor, 8:9, :] = jnp.broadcast_to(sums["loss"], (1, D))
    VTE[tensor, 9:16, :] = jnp.zeros((7, D), f32)
    early = vector_sum(VTE, VSE, VPE, VDE, True)
    advance(early)

    def progress(i, h):
        if i == first and h == 1:
            zfirst_b(3)
        if i == last and h == 2:
            grad_b(2)

    for i in images:
        ag_forward(3, N4, i)
        ag_wait(3, i)
        if i == last:
            advance(early)
            weight_grad(1, ATT, N4)
        b_attention(i, functools.partial(progress, i))
        rs_mid(3, i)
    weight_grad(0, N1, GP)
    b_norm1(first)
    grad_a(1, 3, 1)
    grad_b(1)
    grad_a(0, 3)
    for i in images[1:]:
        b_norm1(i)
    VTL[tensor] = jnp.zeros((8, D), f32)
    VTL[tensor, 0:1, :] = sums["ln1g"]
    VTL[tensor, 1:2, :] = sums["ln1s"]
    VTL[tensor, 2:3, aligned(tensor * HC, HC)] = sums["b_q"]
    VTL[tensor, 3:4, aligned(tensor * HC, HC)] = sums["b_v"]
    late = vector_sum(VTL, VSL, VPL, VDL, False)
    advance(late)
    grad_a(0, 1)
    advance(late)
    grad_b(0)
    advance(early)
    zfirst_end(3)
    grad_end(2)
    grad_end(1)

    def cut(V, row, count):
        part = V[8, row:row + count, :]
        picked = jnp.zeros((count, 32), f32)
        for t in range(4):
            picked = jnp.where(tensor == t, part[:, 32 * t:32 * t + 32], picked)
        return picked

    if inside:
        small[...] = jnp.zeros(small.shape, f32)
        small[0:1, :] = VDE[8, 0:1, :]
        small[1:5, 0:32] = cut(VDE, 4, 4)
        small[5:6, :] = VDE[8, 8:9, :] / normalizer
        advance(late)
        small[6:10, 0:32] = cut(VDL, 0, 4)
    else:
        small[0:16, :] = VSE[...]
        small[8:9, :] = VSE[8:9, :] / normalizer
        small[16:24, :] = VSL[...]
    grad_end(0)
    net.finish()


def finish_kernel(*refs):
    small, big = refs[0], refs[1:7]
    results, sem = refs[7:-1], refs[-1]
    copies = [pltpu.make_async_copy(src, dst, sem.at[n]) for n, (src, dst) in enumerate(zip(big, results[:6]))]
    for copy in copies:
        copy.start()
    units, loss, rest = results[6], results[7], results[8:]
    units[...] = small[0:1, :]
    loss[...] = small[5:6, 0:1]
    row = 1
    for ref in rest:
        count, width = ref.shape
        ref[...] = small[row:row + count, 0:width]
        row += count + (1 if row + count == 5 else 0)
    for copy in copies:
        copy.wait()


def finish(small, big, width):
    vm, hbm = pl.BlockSpec(memory_space=pltpu.VMEM), pl.BlockSpec(memory_space=pl.ANY)
    shape = jax.ShapeDtypeStruct
    vectors = [(1, 128), (1, 1)] + [(1, width)] * 6 + [(2, width)]
    return pl.pallas_call(
        finish_kernel,
        out_shape=[shape(v.shape, v.dtype) for v in big] + [shape(v, f32) for v in vectors],
        in_specs=[vm] * 7,
        out_specs=[hbm] * 6 + [vm] * 9,
        scratch_shapes=[pltpu.SemaphoreType.DMA((6,))],
        compiler_params=pltpu.CompilerParams(vmem_limit_bytes=60 * 2 ** 20),
    )(small, *big)


def body(
    mesh_dp, tokens, valid_mask, teacher, loss_scale, ln1_gain, ln1_shift, w_qkv, b_qv, w_out, b_out,
    ln2_gain, ln2_shift, w_fc1, b_fc1, w_fc2, b_fc2,
):
    rows, I, D = tokens.shape
    seq = valid_mask.shape[0]
    parts = seq // rows
    HC, UC = w_qkv.shape[2], w_fc1.shape[1]
    LR = -(-rows // 16) * 16
    IR = parts * LR
    inside = mesh_dp == 8
    part = lax.axis_index("tensor")

    NB = D // 128
    if inside:
        count = loss_scale
        weights = (jnp.transpose(w_qkv, (1, 0, 2)), w_out, w_fc1, w_fc2)
        gdt = f32
    else:
        count = lax.psum(jnp.sum(valid_mask.astype(f32)), "dp")

        def blocks(values):
            full = lax.all_gather(values, "dp", axis=1, tiled=True)
            return jnp.transpose(full.reshape(-1, NB, 128), (1, 0, 2))

        weights = (
            jnp.transpose(lax.all_gather(w_qkv, "dp", axis=0, tiled=True), (1, 0, 2)),
            blocks(w_out),
            lax.all_gather(w_fc1, "dp", axis=0, tiled=True),
            blocks(w_fc2),
        )
        gdt = bf16
    KS = w_fc1.shape[0]
    flat = [v.reshape(1, -1) for v in (ln1_gain, ln1_shift, ln2_gain, ln2_shift, b_out, b_fc2, b_fc1)]
    size = dict(I=I, LR=LR, SR=rows, IR=IR, D=D, HC=HC, UC=UC, KS=KS, inside=inside)
    H = HC // HD
    VM = pltpu.VMEM
    if inside:
        gshapes = [(3, KS, HC), (HC, KS), (KS, UC), (UC, KS)]
    else:
        gshapes = [(3, D, HC), (NB, HC, 128), (D, UC), (NB, UC, 128)]
    k4, k3 = (4, 3) if inside else (1, 1)
    part_shapes = gshapes if inside else [(16, 128)] * 4
    scratch = [
        VM((3, D, HC), bf16), VM((NB, HC, 128), bf16), VM((D, UC), bf16), VM((NB, UC, 128), bf16),
        VM((I * IR, D), bf16), VM((I * IR, D), bf16), VM((I * IR, D), bf16), VM((I * IR, D), bf16),
        VM((I * IR, 3 * HC), bf16), VM((I * H, IR, IR), bf16), VM((I * IR, HC), bf16),
        VM((I * IR, UC), bf16), VM((I * IR, UC), bf16), VM((IR, HC), bf16), VM((I * IR, 3 * HC), bf16),
        VM((I * IR, D), bf16), VM((2 * I * LR, D), bf16), VM((I * LR, D), bf16), VM((I * LR, D), bf16),
        VM((I * LR, D), f32), VM((I * LR, D), f32),
        VM((3, D, HC), bf16), VM((NB, HC, 128), bf16), VM((D, UC), bf16), VM((NB, UC, 128), bf16),
    ]
    scratch += [VM((k4,) + s, bf16) for s in part_shapes]
    scratch += [VM((k3,) + s, bf16) for s in part_shapes]
    scratch += [
        VM((I * LR, D), bf16), VM((8, IR), f32), VM((I * LR, 128), f32), VM((8, UC), f32),
        VM((4, 16, D), f32), VM((16, D), f32), VM((8, 16, 128), f32), VM((9, 16, 128), f32),
        VM((4, 8, D), f32), VM((8, D), f32), VM((8, 8, 128), f32), VM((9, 8, 128), f32),
        VM((6, 8, 128), f32),
        pltpu.SemaphoreType.DMA((4,)), pltpu.SemaphoreType.DMA((150,)), pltpu.SemaphoreType.DMA((150,)),
    ]
    vm, hbm = pl.BlockSpec(memory_space=pltpu.VMEM), pl.BlockSpec(memory_space=pl.ANY)
    shape = jax.ShapeDtypeStruct
    results = pl.pallas_call(
        functools.partial(kernel, size),
        out_shape=[shape((rows, I, D), bf16), shape((rows, I, D), f32)]
        + [shape(s, gdt) for s in gshapes]
        + [shape((16, 128) if inside else (24, D), f32)],
        in_specs=[vm] * 13 + [hbm] * 4,
        out_specs=[vm] * 7,
        scratch_shapes=scratch,
        compiler_params=pltpu.CompilerParams(
            collective_id=0, has_side_effects=True, vmem_limit_bytes=64 * 2 ** 20 - 2 ** 16
        ),
    )(tokens, teacher, valid_mask.T, *flat, b_qv, loss_scale.reshape(1, 1), count.reshape(1, 1), *weights)
    out, gtok, gq, go, g1, g2, small = results

    n = D // (mesh_dp * parts)
    if inside:
        out, gtok, gq, go, g1, g2, units, loss, s2g, s2s, sb2, sbo, s1g, s1s, sqv = finish(
            small, (out, gtok, gq, go, g1, g2), n
        )
        return (
            out, loss[0, 0], gtok, s1g[0], s1s[0], jnp.transpose(gq, (1, 0, 2)), sqv, go, sbo[0],
            s2g[0], s2s[0], g1, units[0], g2, sb2[0],
        )
    gq = jnp.transpose(gq, (1, 0, 2))
    if not inside:
        def whole(values):
            full = jnp.transpose(values, (1, 0, 2)).reshape(-1, D)
            return lax.psum_scatter(full, "dp", scatter_dimension=1, tiled=True).astype(f32)

        index = lax.axis_index("dp") * parts + part
        gq = lax.psum_scatter(gq, "dp", scatter_dimension=0, tiled=True).astype(f32)
        g1 = lax.psum_scatter(g1, "dp", scatter_dimension=0, tiled=True).astype(f32)
        go, g2 = whole(go), whole(g2)
        small = lax.psum(small, "dp")
        cut = lax.dynamic_slice_in_dim(small, index * n, n, 1)
        cut = jnp.concatenate([cut[3:9], cut[16:20]], axis=0)
        m = UC // mesh_dp
        units_cut = lax.dynamic_slice_in_dim(small[0:parts].reshape(-1), index * m, m, 0)
    return (
        out, small[8, 0], gtok, cut[6], cut[7], gq, cut[8:10], go,
        cut[4], cut[1], cut[2], g1, units_cut, g2, cut[3],
    )


def solution(mesh):
    in_specs = (
        P("tensor", "dp", None), P(None, "dp"), P("tensor", "dp", None), P(), P(), P(),
        P("dp", None, "tensor"), P(), P("tensor", "dp"), P(), P(), P(), P("dp", "tensor"), P(),
        P("tensor", "dp"), P(),
    )
    both = ("dp", "tensor")
    out_specs = (
        P("tensor", "dp", None), P(), P("tensor", "dp", None), P(both), P(both), P("dp", None, "tensor"),
        P(None, both), P("tensor", "dp"), P(both), P(both), P(both), P("dp", "tensor"), P(both),
        P("tensor", "dp"), P(both),
    )
    return jax.shard_map(
        functools.partial(body, mesh.shape["dp"]), mesh=mesh, in_specs=in_specs, out_specs=out_specs,
        check_vma=False,
    )
```

```python
import functools

import jax
import jax.numpy as jnp
from jax import lax
from jax.experimental import pallas as pl
from jax.experimental.pallas import tpu as pltpu
from jax.sharding import PartitionSpec as P

HD = 64
EPS = 1e-05
MASKED = -1000000000.0
PADDED = -3000000000.0
GELU = 1.702
MESH = pl.DeviceIdType.MESH
f32 = jnp.float32
bf16 = jnp.bfloat16
NN = (((1,), (0,)), ((), ()))
NT = (((1,), (1,)), ((), ()))
TN = (((0,), (0,)), ((), ()))

def dot(a, b, dims):
    return lax.dot_general(a, b, dims, preferred_element_type=f32)


def layer_norm(values, gain, shift):
    center = values - jnp.mean(values, axis=-1, keepdims=True)
    inverse = lax.rsqrt(jnp.mean(center * center, axis=-1, keepdims=True) + EPS)
    scaled = center * inverse
    return scaled * gain + shift, scaled, inverse


def norm_backward(upstream, scaled, inverse, gain):
    weighted = upstream * gain
    inner = weighted - jnp.mean(weighted, axis=-1, keepdims=True)
    inner = inner - scaled * jnp.mean(weighted * scaled, axis=-1, keepdims=True)
    return inverse * inner


def rowsum(values):
    return jnp.sum(values, axis=0, keepdims=True)


def aligned(start, size):
    if isinstance(start, int):
        return pl.ds(start, size)
    return pl.ds(pl.multiple_of(start, size), size)


class Copies:
    def __init__(self, send, recv):
        self.send, self.recv, self.count = send, recv, 0
        self.all = []

    def make(self, src, dst, device):
        copy = pltpu.make_async_remote_copy(
            src_ref=src,
            dst_ref=dst,
            send_sem=self.send.at[self.count],
            recv_sem=self.recv.at[self.count],
            device_id=device,
            device_id_type=MESH,
        )
        self.count += 1
        return copy

    def start(self, src, dst, device):
        copy = self.make(src, dst, device)
        copy.start()
        self.all.append(copy)
        return copy

    def wait_send(self, copy):
        copy.wait_send()
        self.all = [other for other in self.all if other is not copy]

    def finish(self):
        for copy in self.all:
            copy.wait_send()
        self.all = []


def kernel(
    size,
    tok, tea, mask, ln1g, ln1s, ln2g, ln2s, bout, bfc2, bfc1, bqv, lscale, given, wq, wo, w1, w2,
    out_h, gtok_h, gq_h, go_h, g1_h, g2_h, small,
    Wq, Wo, W1, W2, N1, N2, N3, N4, QKV, PR, ATT, ACT, DAC, GA, GP, PART, RA, RX, XS, MID, DIF,
    GWq, GWo, GW1, GW2, YRq, YRo, YR1, YR2, ZRq, ZRo, ZR1, ZR2,
    TOK, KEEP, RM, USUM, out, gtok, gq, go, g1, g2, VTE, VSE, VPE, VDE, VTL, VSL, VPL, VDL, CN, local_sem, send_sem, recv_sem,
):
    I, LR, IR, D, HC, UC = size["I"], size["LR"], size["IR"], size["D"], size["HC"], size["UC"]
    inside = size["inside"]
    KS, SR = size["KS"], size["SR"]
    dp, tensor = lax.axis_index("dp"), lax.axis_index("tensor")
    z, y, x, c = dp // 2, dp % 2, tensor // 2, tensor % 2
    mate = (dp, x * 2 + 1 - c)
    xnei = (dp, (1 - x) * 2 + c)
    diag = (dp, (1 - x) * 2 + 1 - c)
    ynei = (z * 2 + 1 - y, tensor)

    def zat(k):
        return (z, z + 1 - 2 * (z % 2), lax.rem(z + 2, 4), 3 - z)[k]

    def zdev(k):
        return (zat(k) * 2 + y, tensor)

    net = Copies(send_sem, recv_sem)
    leaving = []

    def leave(n):
        src, dst = ((out, out_h), (gtok, gtok_h), (gq, gq_h), (go, go_h), (g1, g1_h), (g2, g2_h))[n]
        copy = pltpu.make_async_copy(src, dst, local_sem.at[4 + n])
        copy.start()
        leaving.append(copy)


    barrier = pltpu.get_barrier_semaphore()
    group = [zat(k) * 2 + y for k in (1, 2, 3)] + [zat(k) * 2 + 1 - y for k in (0, 1, 2, 3)]
    peers = [mate, xnei, diag] + ([(other, tensor) for other in group] if inside else [])
    for peer in peers:
        pl.semaphore_signal(barrier, inc=1, device_id=peer, device_id_type=MESH)
    pl.semaphore_wait(barrier, len(peers))

    weights = [(wq, Wq, 0, YRq, ZRq, GWq, gq), (wo, Wo, 1, YRo, ZRo, GWo, go),
               (w1, W1, 2, YR1, ZR1, GW1, g1), (w2, W2, 1, YR2, ZR2, GW2, g2)]

    def shard(ref, kind, index):
        if kind == 1:
            return ref.at[index]
        place = pl.ds(pl.multiple_of(index * KS, KS), KS)
        return ref.at[:, place, :] if kind == 0 else ref.at[place, :]

    def columns(ref, start, count, rows=slice(None)):
        return jnp.concatenate([ref[n, rows, :] for n in range(start // 128, (start + count) // 128)], axis=1)

    gathers = {}
    locals_ = []

    def weight_send(w):
        arg, full, axis = weights[w][:3]
        mine = shard(full, axis, dp) if inside else full
        copy = pltpu.make_async_copy(arg, mine, local_sem.at[w])
        copy.start()
        locals_.append(copy)
        if inside:
            gathers[w] = {k: net.start(arg, mine, zdev(k)) for k in (1, 2, 3)}, {}

    def weight_own(w):
        if inside:
            arg, full, axis = weights[w][:3]
            gathers[w][1][0] = net.start(arg, shard(full, axis, dp), ynei)

    def weight_forward(w, *ks):
        if not inside:
            return
        full, axis = weights[w][1:3]
        zs, ys = gathers[w]
        for k in ks:
            zs[k].wait_recv()
            got = shard(full, axis, zat(k) * 2 + y)
            ys[k] = net.start(got, got, ynei)

    def weight_wait(w, *ks):
        ks = ks or (0, 1, 2, 3)
        if 0 in ks:
            locals_[w].wait()
        if inside:
            for k in ks:
                gathers[w][1][k].wait_recv()

    scatters = {w: ({}, {}) for w in range(4)}
    order = (3, 1, 2, 0)

    def grad_y(w, k):
        if inside:
            axis, YR, GW = weights[w][2], weights[w][3], weights[w][5]
            scatters[w][0][k] = net.start(shard(GW, axis, zat(k) * 2 + 1 - y), YR.at[k], ynei)

    def weight_grad(w, lhs, rhs, hold=()):
        GW = weights[w][5]
        step = D // 4
        for k in order:
            group = zat(k) if inside else k
            place = aligned(group * step, step)
            if w == 0:
                part = dot(lhs[:, place], rhs[...], TN).astype(bf16)
                for n in range(3):
                    GW[n, place, :] = part[:, n * HC:(n + 1) * HC]
            elif w == 2:
                GW[place, :] = dot(lhs[:, place], rhs[...], TN).astype(bf16)
            else:
                part = dot(lhs[...], rhs[:, place], TN).astype(bf16)
                GW[group * 2] = part[:, :128]
                GW[group * 2 + 1] = part[:, 128:]
            if k not in hold:
                grad_y(w, k)

    def zfirst_send(w):
        if inside:
            axis, YR, GW = weights[w][2], weights[w][3], weights[w][5]
            for yy, slot in ((1 - y, 0), (y, 1)):
                for k in (3, 1):
                    part = shard(GW, axis, zat(k) * 2 + yy)
                    place = YR.at[(0 if k == 3 else 2) + slot]
                    scatters[w][0][k, slot] = net.start(part, place, zdev(1))

    def zfirst_a(w, k):
        if not inside:
            return
        axis, YR, ZR, GW = weights[w][2:6]
        scatters[w][0][1 + k, 0].wait_recv()
        place = shard(GW, axis, zat(k) * 2 + 1 - y)
        place[...] = (place[...].astype(f32) + YR[2 - k].astype(f32)).astype(bf16)
        scatters[w][1][k] = net.start(place, ZR.at[1 - k // 2], ynei)

    def zfirst_b(w):
        if not inside:
            return
        axis, YR, ZR, GW = weights[w][2:6]
        scatters[w][0][3, 1].wait_recv()
        scatters[w][1][2].wait_recv()
        place = shard(GW, axis, zat(2) * 2 + y)
        total = place[...].astype(f32) + YR[1].astype(f32) + ZR[0].astype(f32)
        place[...] = total.astype(bf16)
        scatters[w][1][3] = net.start(place, ZR.at[2], zdev(2))

    def zfirst_end(w):
        axis, YR, ZR, GW, result = weights[w][2:7]
        if not inside:
            result[...] = GW[...]
            return
        scatters[w][0][1, 1].wait_recv()
        scatters[w][1][0].wait_recv()
        scatters[w][1][3].wait_recv()
        total = shard(GW, axis, dp)[...].astype(f32) + YR[3].astype(f32)
        result[...] = total + ZR[1].astype(f32) + ZR[2].astype(f32)

    def grad_a(w, *ks):
        if not inside:
            return
        axis, YR, ZR, GW = weights[w][2:6]
        for k in ks:
            scatters[w][0][k].wait_recv()
            place = shard(GW, axis, zat(k) * 2 + y)
            place[...] = (place[...].astype(f32) + YR[k].astype(f32)).astype(bf16)
            scatters[w][1][k] = net.start(place, ZR.at[k // 2], zdev(1))

    def grad_b(w):
        if not inside:
            return
        axis, YR, ZR, GW = weights[w][2:6]
        scatters[w][0][2].wait_recv()
        scatters[w][1][3].wait_recv()
        place = shard(GW, axis, zat(2) * 2 + y)
        total = place[...].astype(f32) + YR[2].astype(f32) + ZR[1].astype(f32)
        place[...] = total.astype(bf16)
        scatters[w][1][2] = net.start(place, ZR.at[2], zdev(2))

    def grad_end(w):
        axis, YR, ZR, GW, result = weights[w][2:7]
        if not inside:
            result[...] = GW[...]
            return
        scatters[w][0][0].wait_recv()
        scatters[w][1][1].wait_recv()
        scatters[w][1][2].wait_recv()
        total = shard(GW, axis, dp)[...].astype(f32) + YR[0].astype(f32)
        result[...] = total + ZR[0].astype(f32) + ZR[2].astype(f32)

    def vector_sum(VT, VS, VP, VD, units):
        copies = [net.start(VT.at[tensor], VT.at[tensor], peer) for peer in (mate, xnei, diag)]
        yield
        for copy in copies:
            copy.wait_recv()
        VS[...] = (VT[0] + VT[1]) + (VT[2] + VT[3])
        if not inside:
            return
        for d in range(8):
            VP[d] = VS[:, d * 128:(d + 1) * 128]
            if units:
                VP[d, 0:1, :] = VS[d // 2:d // 2 + 1, aligned((d % 2 * 4 + tensor) * 128, 128)]
        VD[dp] = VP[dp]
        copies = [net.start(VP.at[other], VD.at[dp], (other, tensor)) for other in group]
        yield
        for copy in copies:
            copy.wait_recv()
        VD[8] = ((VD[0] + VD[1]) + (VD[2] + VD[3])) + ((VD[4] + VD[5]) + (VD[6] + VD[7]))

    def advance(steps):
        next(steps, None)

    def count_start():
        if not inside:
            return None
        CN[z] = jnp.broadcast_to(jnp.sum(mask[...].astype(f32), keepdims=True), (8, 128))
        return [net.start(CN.at[z], CN.at[z], zdev(k)) for k in (1, 2, 3)]

    def count_next(copies):
        if not inside:
            return None
        for copy in copies:
            copy.wait_recv()
        CN[4] = (CN[0] + CN[1]) + (CN[2] + CN[3])
        return net.start(CN.at[4], CN.at[5], ynei)

    def count_end(copy):
        if not inside:
            return given[...]
        copy.wait_recv()
        return CN[4, 0:1, 0:1] + CN[5, 0:1, 0:1]

    def block(i, t):
        return aligned((i * 4 + t) * LR, LR)

    def local(i):
        return pl.ds(i * LR, LR)

    def pair(i, xx):
        return aligned(i * IR + xx * 2 * LR, 2 * LR)

    own_t, other_t = tensor, (1 - x) * 2 + c
    ag, rs = {}, {}

    def ag_start(s, N, i):
        mine = N.at[block(i, own_t), :]
        ag[s, i] = [net.start(mine, mine, xnei), net.start(mine, mine, mate)]

    def ag_forward(s, N, i):
        ag[s, i][0].wait_recv()
        got = N.at[block(i, other_t), :]
        ag[s, i].append(net.start(got, got, mate))

    def ag_wait(s, i):
        ag[s, i][1].wait_recv()
        ag[s, i][2].wait_recv()

    def landing(ref, n):
        return ref.at[pl.ds(n * LR, LR), :]

    half = (z // 2) if inside else 0
    early_cols, late_cols = aligned(half * (D // 2), D // 2), aligned((1 - half) * (D // 2), D // 2)
    all_cols = pl.ds(0, D)

    def rs_ready(s, i):
        for copies in rs.get((s - 1, i), []):
            for copy in copies[:2]:
                net.wait_send(copy)

    def rs_send(s, i, far, cols=all_cols):
        base = i * IR + ((1 - x) if far else x) * 2 * LR
        src = PART.at[aligned(base + (1 - c) * LR, LR), cols]
        dst = RA.at[pl.ds((i * 2 + (0 if far else 1)) * LR, LR), cols]
        if far:
            rs.setdefault((s, i), []).append([])
        rs[s, i][-1].append(net.start(src, dst, mate))

    def rs_mid(s, i, cols=all_cols):
        copies = rs[s, i][-1]
        copies[0].wait_recv()
        if len(rs[s, i]) == 1:
            for before in rs.get((s - 1, i), []):
                net.wait_send(before[2])
        kept = PART[aligned(i * IR + (1 - x) * 2 * LR + c * LR, LR), cols]
        got = RA[pl.ds(i * 2 * LR, LR), cols]
        XS[local(i), cols] = (kept.astype(f32) + got.astype(f32)).astype(bf16)
        copies.append(net.start(XS.at[local(i), cols], RX.at[local(i), cols], xnei))

    def rs_finish(s, i):
        for copies in rs[s, i]:
            copies[1].wait_recv()
            copies[2].wait_recv()
        kept = PART[aligned(i * IR + x * 2 * LR + c * LR, LR), :].astype(f32)
        return kept + landing(RA, i * 2 + 1)[...].astype(f32) + RX[local(i), :].astype(f32)

    def prepare_teacher(i):
        start = (i * 4 + own_t) * LR
        N3[aligned(start + SR // 16 * 16, 16), :] = jnp.zeros((16, D), bf16)
        N3[pl.ds(pl.multiple_of(start, LR), SR), :] = tea[:, i, :]

    def prepare_masks():
        KEEP[...] = jnp.zeros(KEEP.shape, f32)
        for t in range(4):
            KEEP[0:I, t * LR:t * LR + SR] = mask[:, t * SR:(t + 1) * SR].astype(f32)
        near = lax.broadcasted_iota(jnp.int32, (LR, LR), 0) == lax.broadcasted_iota(jnp.int32, (LR, LR), 1)
        for i in range(I):
            row = jnp.zeros((1, LR), f32)
            for t in range(4):
                row = jnp.where(tensor == t, KEEP[i:i + 1, t * LR:(t + 1) * LR], row)
            RM[local(i), 0:1] = jnp.sum(jnp.where(near, row, 0.0), axis=1, keepdims=True)

    TC = 512 if D % 512 == 0 and UC % 512 == 0 else 256

    def over_columns(n, step, body):
        for j in range(n // step):
            body(pl.ds(j * step, step))

    def f_norm1(i):
        TOK[i * LR + SR // 16 * 16:(i + 1) * LR, :] = jnp.zeros((LR - SR // 16 * 16, D), bf16)
        TOK[i * LR:i * LR + SR, :] = tok[:, i, :]
        normed = layer_norm(TOK[local(i), :].astype(f32), ln1g[...], ln1s[...])[0]
        N1[block(i, own_t), :] = normed.astype(bf16)
        ag_start(0, N1, i)

    lane_head = lax.broadcasted_iota(jnp.int32, (1, HC), 1) // HD
    zero = jnp.zeros((), bf16)

    def f_attention(i, before_heads, before_out):
        rows = pl.ds(i * IR, IR)
        place = aligned(tensor * HC, HC)
        for n in range(3):
            proj = dot(N1[rows, :], Wq[n], NN)
            if n == 0:
                proj = (proj + bqv[0:1, place]).astype(bf16).astype(f32) * (HD ** -0.5)
            elif n == 2:
                proj = proj + bqv[1:2, place]
            QKV[rows, n * HC:(n + 1) * HC] = proj.astype(bf16)
        before_heads()
        acc = None
        kept = KEEP[i:i + 1, :]
        real = lax.broadcasted_iota(jnp.int32, (1, IR), 1) % LR < SR
        bias = jnp.where(kept > 0.0, 0.0, jnp.where(real, MASKED, PADDED))
        for h in range(HC // HD):
            pick = lane_head == h
            keys = jnp.where(pick, QKV[rows, HC:2 * HC], zero)
            scores = dot(QKV[rows, 0:HC], keys, NT)
            scores = scores * kept + bias
            expo = jnp.exp(scores - jnp.max(scores, axis=-1, keepdims=True))
            probs = (expo * (1.0 / jnp.sum(expo, axis=-1, keepdims=True))).astype(bf16)
            PR[i * (HC // HD) + h] = probs
            values = jnp.where(pick, QKV[rows, 2 * HC:3 * HC], zero)
            part = dot(probs, values, NN)
            acc = part if acc is None else acc + part
        ATT[rows, :] = acc.astype(bf16)
        before_out()
        rs_ready(0, i)
        for far in (True, False):
            prow = pair(i, (1 - x) if far else x)
            def body(cols):
                PART[prow, cols] = dot(ATT[prow, :], columns(Wo, cols.start, cols.size), NN).astype(bf16)
            over_columns(D, TC, body)
            rs_send(0, i, far)

    def f_norm2(i):
        middle = TOK[local(i), :].astype(f32) + rs_finish(0, i) + bout[...]
        MID[local(i), :] = middle
        N2[block(i, own_t), :] = layer_norm(middle, ln2g[...], ln2s[...])[0].astype(bf16)
        ag_start(1, N2, i)

    def f_feed(i):
        rows = pl.ds(i * IR, IR)
        ag_wait(1, i)
        def body(cols):
            pre = dot(N2[rows, :], W1[:, cols], NN) + bfc1[0:1, aligned(tensor * UC + cols.start, cols.size)]
            sigma = jax.nn.sigmoid(GELU * pre)
            act = pre * sigma
            ACT[rows, cols] = act.astype(bf16)
            DAC[rows, cols] = (sigma + GELU * act * (1.0 - sigma)).astype(bf16)
        over_columns(UC, 256, body)

    def f_feed_out(i, late):
        if not late:
            rs_ready(1, i)
        cols = late_cols if late else early_cols
        first_block = ((1 - half) if late else half) * (D // 256)
        blocks = jnp.concatenate([W2[first_block + n] for n in range(D // 256)], axis=1)
        for far in (True, False):
            prow = pair(i, (1 - x) if far else x)
            PART[prow, cols] = dot(ACT[prow, :], blocks, NN).astype(bf16)
            rs_send(1, i, far, cols)

    sums = {}

    def add(name, value):
        sums[name] = value if name not in sums else sums[name] + value

    def f_final(i, factor):
        final = MID[local(i), :] + rs_finish(1, i) + bfc2[...]
        out[:, i, :] = final[:SR].astype(bf16)
        difference = final - N3[block(i, own_t), :].astype(f32)
        masked = difference * RM[local(i), 0:1]
        add("loss", jnp.sum(jnp.sum(masked * difference, axis=0, keepdims=True), axis=1, keepdims=True))
        grad_final = masked * factor
        DIF[local(i), :] = grad_final
        add("b_fc2", rowsum(grad_final))
        N3[block(i, own_t), :] = grad_final.astype(bf16)
        ag_start(2, N3, i)

    def b_feed(i):
        rows = pl.ds(i * IR, IR)
        def body(cols):
            grad = dot(N3[rows, :], columns(W2, 0, D, cols), NT) * DAC[rows, cols].astype(f32)
            grad = grad.astype(bf16)
            DAC[rows, cols] = grad
            total = rowsum(grad.astype(f32))
            USUM[0:1, cols] = total if i == 0 else USUM[0:1, cols] + total
        over_columns(UC, 256, body)
        rs_ready(2, i)
        for far in (True, False):
            prow = pair(i, (1 - x) if far else x)
            def body2(cols):
                PART[prow, cols] = dot(DAC[prow, :], W1[cols, :], NT).astype(bf16)
            over_columns(D, TC, body2)
            rs_send(2, i, far)

    def b_norm2(i):
        middle = MID[local(i), :]
        _, scaled, inverse = layer_norm(middle, ln2g[...], ln2s[...])
        upstream = rs_finish(2, i)
        add("ln2g", rowsum(upstream * scaled))
        add("ln2s", rowsum(upstream))
        grad_middle = DIF[local(i), :] + norm_backward(upstream, scaled, inverse, ln2g[...])
        DIF[local(i), :] = grad_middle
        add("b_out", rowsum(grad_middle))
        N4[block(i, own_t), :] = grad_middle.astype(bf16)
        ag_start(3, N4, i)

    def b_attention(i, before_head):
        rows = pl.ds(i * IR, IR)
        GA[...] = dot(N4[rows, :], columns(Wo, 0, D), NT).astype(bf16)
        grad = GA[...]
        weighed = grad.astype(f32) * ATT[rows, :].astype(f32)
        query_t = QKV[rows, 0:HC].T
        grad_t = grad.T
        acc, keys_t, values_t = None, [], []
        for h in range(HC // HD):
            pick = lane_head == h
            before_head(h)
            row_dot = jnp.sum(jnp.where(pick, weighed, 0.0), axis=-1, keepdims=True)
            values = jnp.where(pick, QKV[rows, 2 * HC:3 * HC], zero)
            grad_probs = dot(grad, values, NT)
            probs = PR[i * (HC // HD) + h]
            grad_scores = (probs.astype(f32) * ((grad_probs - row_dot) * KEEP[i:i + 1, :])).astype(bf16)
            keys = jnp.where(pick, QKV[rows, HC:2 * HC], zero)
            part = dot(grad_scores, keys, NN)
            acc = part if acc is None else acc + part
            keys_t.append(dot(query_t[h * HD:(h + 1) * HD, :], grad_scores, NN))
            values_t.append(dot(grad_t[h * HD:(h + 1) * HD, :], probs, NN))
        grad_query = (acc * (HD ** -0.5)).astype(bf16)
        grad_key = jnp.concatenate(keys_t, axis=0).astype(bf16).T
        grad_value = jnp.concatenate(values_t, axis=0).astype(bf16).T
        GP[rows, 0:HC] = grad_query
        GP[rows, HC:2 * HC] = grad_key
        GP[rows, 2 * HC:3 * HC] = grad_value
        add("b_q", rowsum(grad_query.astype(f32)))
        add("b_v", rowsum(grad_value.astype(f32)))

    def b_attention_out(i):
        rs_ready(3, i)
        for far in (True, False):
            prow = pair(i, (1 - x) if far else x)
            def body2(cols):
                PART[prow, cols] = dot(GP[prow, :], jnp.concatenate([Wq[n, cols, :] for n in range(3)], axis=1), NT).astype(bf16)
            over_columns(D, TC, body2)
            rs_send(3, i, far)

    def b_norm1(i):
        _, scaled, inverse = layer_norm(TOK[local(i), :].astype(f32), ln1g[...], ln1s[...])
        upstream = rs_finish(3, i)
        add("ln1g", rowsum(upstream * scaled))
        add("ln1s", rowsum(upstream))
        grad = DIF[local(i), :] + norm_backward(upstream, scaled, inverse, ln1g[...])
        gtok[:, i, :] = grad[:SR]

    def nothing():
        pass

    images = list(range(I))
    first, last = images[0], images[-1]
    counting = count_start()
    weight_send(0)
    weight_own(0)
    weight_send(1)
    weight_send(2)
    weight_send(3)
    for i in images:
        f_norm1(i)
    prepare_masks()
    for i in images:
        prepare_teacher(i)
    weight_forward(0, 1)
    ag_forward(0, N1, first)
    weight_forward(0, 2)
    for i in images[1:]:
        ag_forward(0, N1, i)
    weight_forward(0, 3)
    weight_own(1)
    weight_wait(0)

    def out_forward():
        weight_forward(1, 1, 2, 3)
        weight_own(2)
        weight_own(3)

    for i in images:
        ag_wait(0, i)
        if i == first:
            f_attention(i, out_forward, lambda: weight_wait(1))
        else:
            f_attention(i, nothing, nothing)
        rs_mid(0, i)
        if i == first:
            weight_forward(2, 1)
    weight_forward(2, 2)
    f_norm2(first)
    weight_forward(2, 3)
    for i in images[1:]:
        f_norm2(i)
    counting = count_next(counting)
    weight_forward(3, 1)
    ag_forward(1, N2, first)
    weight_wait(2)
    f_feed(first)
    weight_forward(3, 2)
    for i in images[1:]:
        ag_forward(1, N2, i)
        f_feed(i)
    weight_wait(3, 0, 1)
    for i in images:
        f_feed_out(i, False)
        if i == first:
            weight_forward(3, 3)
    for i in images:
        rs_mid(1, i, early_cols)
    weight_wait(3, 2, 3)
    for i in images:
        f_feed_out(i, True)
    for i in images:
        rs_mid(1, i, late_cols)
    count = count_end(counting)
    normalizer = count * float(D)
    factor = lscale[...] * 2.0 / normalizer
    for i in images:
        f_final(i, factor)
    leave(0)
    for i in images:
        ag_forward(2, N3, i)
        ag_wait(2, i)
        if i == last:
            weight_grad(3, ACT, N3, (0, 1, 2, 3))
            zfirst_send(3)
        b_feed(i)
        rs_mid(2, i)
    weight_grad(2, N2, DAC, (2, 0))
    zfirst_a(3, 2)
    b_norm2(first)
    zfirst_a(3, 0)
    grad_y(2, 2)
    grad_y(2, 0)
    for i in images[1:]:
        b_norm2(i)
    grad_a(2, 3, 1)

    for n in range(4):
        VTE[tensor, n:n + 1, :] = jnp.where(tensor == n, USUM[0:1, :], 0.0)
    for n, name in enumerate(("ln2g", "ln2s", "b_fc2", "b_out")):
        VTE[tensor, 4 + n:5 + n, :] = sums[name]
    VTE[tensor, 8:9, :] = jnp.broadcast_to(sums["loss"], (1, D))
    VTE[tensor, 9:16, :] = jnp.zeros((7, D), f32)
    early = vector_sum(VTE, VSE, VPE, VDE, True)
    advance(early)

    def progress(i, h):
        if i == first and h == 1:
            zfirst_b(3)
        if i == last and h == 2:
            grad_b(2)

    for i in images:
        ag_forward(3, N4, i)
        ag_wait(3, i)
        if i == last:
            advance(early)
            weight_grad(1, ATT, N4)
        b_attention(i, functools.partial(progress, i))
        if i == last:
            weight_grad(0, N1, GP)
        b_attention_out(i)
        rs_mid(3, i)
    b_norm1(first)
    grad_a(1, 3, 1)
    grad_b(1)
    for i in images[1:]:
        b_norm1(i)
    leave(1)
    VTL[tensor] = jnp.zeros((8, D), f32)
    VTL[tensor, 0:1, :] = sums["ln1g"]
    VTL[tensor, 1:2, :] = sums["ln1s"]
    VTL[tensor, 2:3, aligned(tensor * HC, HC)] = sums["b_q"]
    VTL[tensor, 3:4, aligned(tensor * HC, HC)] = sums["b_v"]
    late = vector_sum(VTL, VSL, VPL, VDL, False)
    advance(late)
    grad_a(0, 3)
    advance(late)
    grad_a(0, 1)
    grad_b(0)
    advance(early)
    zfirst_end(3)
    leave(5)
    grad_end(2)
    leave(4)
    grad_end(1)
    leave(3)

    def cut(V, row, count):
        part = V[8, row:row + count, :]
        picked = jnp.zeros((count, 32), f32)
        for t in range(4):
            picked = jnp.where(tensor == t, part[:, 32 * t:32 * t + 32], picked)
        return picked

    if inside:
        small[...] = jnp.zeros(small.shape, f32)
        small[0:1, :] = VDE[8, 0:1, :]
        small[1:5, 0:32] = cut(VDE, 4, 4)
        small[5:6, :] = VDE[8, 8:9, :] / normalizer
        advance(late)
        small[6:10, 0:32] = cut(VDL, 0, 4)
    else:
        small[0:16, :] = VSE[...]
        small[8:9, :] = VSE[8:9, :] / normalizer
        small[16:24, :] = VSL[...]
    grad_end(0)
    leave(2)
    net.finish()
    for copy in leaving:
        copy.wait()


def finish_kernel(*refs):
    small, big = refs[0], refs[1:7]
    results, sem = refs[7:-1], refs[-1]
    copies = [pltpu.make_async_copy(src, dst, sem.at[n]) for n, (src, dst) in enumerate(zip(big, results[:6]))]
    for copy in copies:
        copy.start()
    units, loss, rest = results[6], results[7], results[8:]
    units[...] = small[0:1, :]
    loss[...] = small[5:6, 0:1]
    row = 1
    for ref in rest:
        count, width = ref.shape
        ref[...] = small[row:row + count, 0:width]
        row += count + (1 if row + count == 5 else 0)
    for copy in copies:
        copy.wait()


def finish(small, big, width):
    vm, hbm = pl.BlockSpec(memory_space=pltpu.VMEM), pl.BlockSpec(memory_space=pl.ANY)
    shape = jax.ShapeDtypeStruct
    vectors = [(1, 128), (1, 1)] + [(1, width)] * 6 + [(2, width)]
    return pl.pallas_call(
        finish_kernel,
        out_shape=[shape(v.shape, v.dtype) for v in big] + [shape(v, f32) for v in vectors],
        in_specs=[vm] * 7,
        out_specs=[hbm] * 6 + [vm] * 9,
        scratch_shapes=[pltpu.SemaphoreType.DMA((6,))],
        compiler_params=pltpu.CompilerParams(vmem_limit_bytes=60 * 2 ** 20),
    )(small, *big)


def body(
    mesh_dp, tokens, valid_mask, teacher, loss_scale, ln1_gain, ln1_shift, w_qkv, b_qv, w_out, b_out,
    ln2_gain, ln2_shift, w_fc1, b_fc1, w_fc2, b_fc2,
):
    rows, I, D = tokens.shape
    seq = valid_mask.shape[0]
    parts = seq // rows
    HC, UC = w_qkv.shape[2], w_fc1.shape[1]
    LR = -(-rows // 16) * 16
    IR = parts * LR
    inside = mesh_dp == 8
    part = lax.axis_index("tensor")

    NB = D // 128
    if inside:
        count = loss_scale
        weights = (jnp.transpose(w_qkv, (1, 0, 2)), w_out, w_fc1, w_fc2)
        gdt = f32
    else:
        count = lax.psum(jnp.sum(valid_mask.astype(f32)), "dp")

        def blocks(values):
            full = lax.all_gather(values, "dp", axis=1, tiled=True)
            return jnp.transpose(full.reshape(-1, NB, 128), (1, 0, 2))

        weights = (
            jnp.transpose(lax.all_gather(w_qkv, "dp", axis=0, tiled=True), (1, 0, 2)),
            blocks(w_out),
            lax.all_gather(w_fc1, "dp", axis=0, tiled=True),
            blocks(w_fc2),
        )
        gdt = bf16
    KS = w_fc1.shape[0]
    flat = [v.reshape(1, -1) for v in (ln1_gain, ln1_shift, ln2_gain, ln2_shift, b_out, b_fc2, b_fc1)]
    size = dict(I=I, LR=LR, SR=rows, IR=IR, D=D, HC=HC, UC=UC, KS=KS, inside=inside)
    H = HC // HD
    VM = pltpu.VMEM
    if inside:
        gshapes = [(3, KS, HC), (HC, KS), (KS, UC), (UC, KS)]
    else:
        gshapes = [(3, D, HC), (NB, HC, 128), (D, UC), (NB, UC, 128)]
    k4, k3 = (4, 3) if inside else (1, 1)
    part_shapes = gshapes if inside else [(16, 128)] * 4
    scratch = [
        VM((3, D, HC), bf16), VM((NB, HC, 128), bf16), VM((D, UC), bf16), VM((NB, UC, 128), bf16),
        VM((I * IR, D), bf16), VM((I * IR, D), bf16), VM((I * IR, D), bf16), VM((I * IR, D), bf16),
        VM((I * IR, 3 * HC), bf16), VM((I * H, IR, IR), bf16), VM((I * IR, HC), bf16),
        VM((I * IR, UC), bf16), VM((I * IR, UC), bf16), VM((IR, HC), bf16), VM((I * IR, 3 * HC), bf16),
        VM((I * IR, D), bf16), VM((2 * I * LR, D), bf16), VM((I * LR, D), bf16), VM((I * LR, D), bf16),
        VM((I * LR, D), f32), VM((I * LR, D), f32),
        VM((3, D, HC), bf16), VM((NB, HC, 128), bf16), VM((D, UC), bf16), VM((NB, UC, 128), bf16),
    ]
    scratch += [VM((k4,) + s, bf16) for s in part_shapes]
    scratch += [VM((k3,) + s, bf16) for s in part_shapes]
    scratch += [
        VM((I * LR, D), bf16), VM((8, IR), f32), VM((I * LR, 128), f32), VM((8, UC), f32),
        VM((rows, I, D), bf16), VM((rows, I, D), f32), *[VM(s, gdt) for s in gshapes],
        VM((4, 16, D), f32), VM((16, D), f32), VM((8, 16, 128), f32), VM((9, 16, 128), f32),
        VM((4, 8, D), f32), VM((8, D), f32), VM((8, 8, 128), f32), VM((9, 8, 128), f32),
        VM((6, 8, 128), f32),
        pltpu.SemaphoreType.DMA((10,)), pltpu.SemaphoreType.DMA((150,)), pltpu.SemaphoreType.DMA((150,)),
    ]
    vm, hbm = pl.BlockSpec(memory_space=pltpu.VMEM), pl.BlockSpec(memory_space=pl.ANY)
    shape = jax.ShapeDtypeStruct
    results = pl.pallas_call(
        functools.partial(kernel, size),
        out_shape=[shape((rows, I, D), bf16), shape((rows, I, D), f32)]
        + [shape(s, gdt) for s in gshapes]
        + [shape((16, 128) if inside else (24, D), f32)],
        in_specs=[vm] * 13 + [hbm] * 4,
        out_specs=[hbm] * 6 + [vm],
        scratch_shapes=scratch,
        compiler_params=pltpu.CompilerParams(
            collective_id=0, has_side_effects=True, vmem_limit_bytes=64 * 2 ** 20 - 2 ** 16
        ),
    )(tokens, teacher, valid_mask.T, *flat, b_qv, loss_scale.reshape(1, 1), count.reshape(1, 1), *weights)
    out, gtok, gq, go, g1, g2, small = results

    n = D // (mesh_dp * parts)
    if inside:
        out, gtok, gq, go, g1, g2, units, loss, s2g, s2s, sb2, sbo, s1g, s1s, sqv = finish(
            small, (out, gtok, gq, go, g1, g2), n
        )
        return (
            out, loss[0, 0], gtok, s1g[0], s1s[0], jnp.transpose(gq, (1, 0, 2)), sqv, go, sbo[0],
            s2g[0], s2s[0], g1, units[0], g2, sb2[0],
        )
    gq = jnp.transpose(gq, (1, 0, 2))
    if not inside:
        def whole(values):
            full = jnp.transpose(values, (1, 0, 2)).reshape(-1, D)
            return lax.psum_scatter(full, "dp", scatter_dimension=1, tiled=True).astype(f32)

        index = lax.axis_index("dp") * parts + part
        gq = lax.psum_scatter(gq, "dp", scatter_dimension=0, tiled=True).astype(f32)
        g1 = lax.psum_scatter(g1, "dp", scatter_dimension=0, tiled=True).astype(f32)
        go, g2 = whole(go), whole(g2)
        small = lax.psum(small, "dp")
        cut = lax.dynamic_slice_in_dim(small, index * n, n, 1)
        cut = jnp.concatenate([cut[3:9], cut[16:20]], axis=0)
        m = UC // mesh_dp
        units_cut = lax.dynamic_slice_in_dim(small[0:parts].reshape(-1), index * m, m, 0)
    return (
        out, small[8, 0], gtok, cut[6], cut[7], gq, cut[8:10], go,
        cut[4], cut[1], cut[2], g1, units_cut, g2, cut[3],
    )


def solution(mesh):
    in_specs = (
        P("tensor", "dp", None), P(None, "dp"), P("tensor", "dp", None), P(), P(), P(),
        P("dp", None, "tensor"), P(), P("tensor", "dp"), P(), P(), P(), P("dp", "tensor"), P(),
        P("tensor", "dp"), P(),
    )
    both = ("dp", "tensor")
    out_specs = (
        P("tensor", "dp", None), P(), P("tensor", "dp", None), P(both), P(both), P("dp", None, "tensor"),
        P(None, both), P("tensor", "dp"), P(both), P(both), P(both), P("dp", "tensor"), P(both),
        P("tensor", "dp"), P(both),
    )
    return jax.shard_map(
        functools.partial(body, mesh.shape["dp"]), mesh=mesh, in_specs=in_specs, out_specs=out_specs,
        check_vma=False,
    )
```
